256 devices in a mesh: grp: 8 (over x, core), row: 32 (over z, y).
Axes of the slice: x: 4, y: 4, z: 8, core: 2. Of those that a mesh axis runs over, the one named last changes fastest.
Arguments:
- a_blocks: bfloat16 [8192, 8, 4096], P(('grp', 'row')), may hold values from -1.1953125 to 1.1953125
- p_blocks: bfloat16 [8192, 4096], P(('grp', 'row')), may hold values from -0.75 to 0.75
- a_cols: int32 [8192, 8], P(('grp', 'row')), may hold values from 0 to 8191, as said below
- a_count: int32 [8192], P(('grp', 'row')), may hold values from 4 to 8
- tile_slot: int32 [8192, 8], P(('grp', 'row')), may hold values from 0 to 2047, as said below
Outputs:
- coarse: float32 [2048, 4096], P(('grp', 'row'))
The draws below stay inside these ranges and needn't reach their ends.
Inputs may be any that keep to these rules, and one draw needn't show every extreme that they name: `a_cols`: A block row held by the device at grp index g and row index r has all its block columns on block rows of devices of grp g, or of the two devices at grp g - 1 and g + 1 (cyclically) with row index r. Among the live entries of one device's block rows, those on another device of the same group name at most 4 distinct block rows of that device, and exactly 4 for some device, for every device. `tile_slot`: every live entry of a block row held in grp g names a coarse block held by a device of grp g, the holder of coarse block s being device s // 8. Among one device's live entries at most 4 distinct coarse blocks are held by any one device, and exactly 4 for some holder, for every device.
All inputs are finite; a program needn't handle non-finite values.
Results may differ from the reference program's by a relative error of at most 0.0029.
Values may be sent and summed in bfloat16 or wider, within the bound.
No kernel may reach another device: no remote copies, remote signals or barrier semaphores. Data moves between devices by JAX's collectives and lax.ppermute only.
A program may use at most 64 MiB of HBM per device.

```python
import jax
import jax.numpy as jnp
from jax import lax

BS = 64
BLOCK_ENTRIES = 4096
ROWS_DEV = 32
KA = 8
CAP = 4
SLOT_DEV = 8
CAP2 = 4
NFB = 8192
COARSE_BLOCKS = 2048
N_GRP = 8
N_ROW = 32


def fine_layout():
    fine_at = jnp.arange(NFB, dtype=jnp.int32)
    dev_at = fine_at // ROWS_DEV
    return (fine_at, dev_at, dev_at // N_ROW, dev_at % N_ROW, fine_at % ROWS_DEV)


def draw_a_cols(key, part):
    key = jax.random.fold_in(key, 11)
    keys = jax.random.split(key, 5)
    fine_at, dev_at, grp_at, row_of, local_at = fine_layout()
    devices = NFB // ROWS_DEV
    scores = jax.random.randint(keys[0], (devices, N_ROW, ROWS_DEV), 0, 65536) * ROWS_DEV + jnp.arange(ROWS_DEV, dtype=jnp.int32)
    chosen = jnp.argsort(scores, axis=-1, stable=True)[:, :, :CAP].astype(jnp.int32)
    below_local = jax.random.randint(keys[1], (NFB,), 0, ROWS_DEV)
    above_local = jnp.where(local_at == ROWS_DEV - 1, ROWS_DEV - 1, jax.random.randint(keys[2], (NFB,), 0, ROWS_DEV))
    below_col = ((grp_at + N_GRP - 1) % N_GRP * N_ROW + row_of) * ROWS_DEV + below_local
    above_col = ((grp_at + 1) % N_GRP * N_ROW + row_of) * ROWS_DEV + above_local
    spread = KA - 3
    offset = jax.random.randint(keys[3], (NFB, spread), 1, N_ROW)
    choice_at = jax.random.randint(keys[4], (NFB, spread), 0, CAP)
    forced = local_at < CAP
    offset = offset.at[:, 0].set(jnp.where(forced, 1, offset[:, 0]))
    choice_at = choice_at.at[:, 0].set(jnp.where(forced, local_at, choice_at[:, 0]))
    peer_at = (row_of[:, None] + offset) % N_ROW
    rows_picked = chosen[dev_at[:, None], peer_at, choice_at]
    inner = (grp_at[:, None] * N_ROW + peer_at) * ROWS_DEV + rows_picked
    return jnp.concatenate([fine_at[:, None], below_col[:, None], above_col[:, None], inner], axis=1).astype(jnp.int32)


def draw_tile_slot(key, part):
    key = jax.random.fold_in(key, 23)
    keys = jax.random.split(key, 5)
    fine_at, dev_at, grp_at, row_of, local_at = fine_layout()
    devices = NFB // ROWS_DEV
    scores = jax.random.randint(keys[0], (devices, N_ROW, SLOT_DEV), 0, 65536) * SLOT_DEV + jnp.arange(SLOT_DEV, dtype=jnp.int32)
    scores = scores.at[:, N_ROW - 1, SLOT_DEV - 1].set(-1)
    scores = scores.at[:, 0, 0].set(-1)
    chosen = jnp.argsort(scores, axis=-1, stable=True)[:, :, :CAP2].astype(jnp.int32)
    hottest = jax.random.randint(keys[1], (N_GRP,), 0, N_ROW)
    coin_at = jax.random.randint(keys[2], (NFB, KA), 0, 2)
    spread_owner = jax.random.randint(keys[3], (NFB, KA), 0, N_ROW)
    owner_at = jnp.where(coin_at == 1, hottest[grp_at][:, None], spread_owner)
    choice_at = jax.random.randint(keys[4], (NFB, KA), 0, CAP2)
    first_owner = jnp.where(local_at < CAP2, hottest[grp_at], owner_at[:, 0])
    first_owner = jnp.where(local_at == ROWS_DEV - 1, N_ROW - 1, first_owner)
    first_owner = jnp.where(local_at == ROWS_DEV - 2, 0, first_owner)
    first_choice = jnp.where(local_at < CAP2, local_at, choice_at[:, 0])
    first_choice = jnp.where(local_at >= ROWS_DEV - 2, 0, first_choice)
    owner_at = owner_at.at[:, 0].set(first_owner)
    choice_at = choice_at.at[:, 0].set(first_choice)
    slot_at = chosen[dev_at[:, None], owner_at, choice_at]
    return ((grp_at[:, None] * N_ROW + owner_at) * SLOT_DEV + slot_at).astype(jnp.int32)


def place_ends(result, key, low, top_value):
    shape = result.shape
    place = [jax.random.randint(jax.random.fold_in(key, axis), (), 0, shape[axis]) for axis in range(len(shape))]
    result = result.at[tuple(place)].set(low)
    longest = shape.index(max(shape))
    place[longest] = (place[longest] + 1) % shape[longest]
    return result.at[tuple(place)].set(top_value)


def levels(rng, extent, cuts, low, largest):
    def one(dim, shards_of):
        heights = jax.random.uniform(jax.random.fold_in(jax.random.fold_in(rng, 6), dim), (shards_of,), jnp.float32, low / len(cuts), largest / len(cuts))
        return jnp.repeat(jnp.exp(heights), extent[dim] // shards_of).reshape((-1,) + (1,) * (len(extent) - dim - 1))

    factor_of = one(*cuts[0])
    for cut in cuts[1:]:
        factor_of = factor_of * one(*cut)
    return factor_of


def noise(stream_key, extent, scale, bound, cuts=(), held_as=jnp.bfloat16):
    gain = levels(stream_key, extent, cuts, -0.22, 0.18) if cuts else 1.0
    entries = jax.random.normal(stream_key, extent, jnp.float32) * scale * gain
    return jnp.minimum(jnp.maximum(entries, -bound), bound).astype(held_as)


def setup_inputs(seed: int = 0) -> dict:
    arg_keys = jax.random.split(jax.random.key(seed), 6)
    a_blocks = noise(arg_keys[0], (NFB, KA, BLOCK_ENTRIES), 0.2, 1.1953125, ((0, 256),))
    p_blocks = noise(arg_keys[1], (NFB, BLOCK_ENTRIES), BS ** -0.5, 0.75, ((0, 256),))
    a_cols = draw_a_cols(jax.random.fold_in(arg_keys[5], 71), 0)
    a_count = place_ends(jax.random.randint(arg_keys[3], (NFB,), 4, KA + 1), jax.random.fold_in(arg_keys[3], 1), 4, KA).astype(jnp.int32)
    tile_slot = draw_tile_slot(jax.random.fold_in(arg_keys[5], 71), 0)
    return {"a_blocks": a_blocks, "p_blocks": p_blocks, "a_cols": a_cols, "a_count": a_count, "tile_slot": tile_slot}


def reference(a_blocks, p_blocks, a_cols, a_count, tile_slot):
    block_count = NFB // ROWS_DEV
    a_split = a_blocks.reshape(block_count, ROWS_DEV, KA, BS, BS)
    col_split = a_cols.reshape(block_count, ROWS_DEV, KA)
    count_split = a_count.reshape(block_count, ROWS_DEV)
    slot_split = tile_slot.reshape(block_count, ROWS_DEV, KA)
    own_split = p_blocks.reshape(block_count, ROWS_DEV, BS, BS)

    def accumulate(grand_total, pieces):
        a_part, col_part, count_part, coarse_slot_part, own_part = pieces
        active_mask = jnp.arange(KA, dtype=jnp.int32)[None, :] < count_part[:, None]
        picked = p_blocks[col_part].reshape(ROWS_DEV, KA, BS, BS).astype(jnp.float32)
        a_times_p = jnp.einsum("rkab,rkbc->rkac", a_part.astype(jnp.float32), picked).astype(jnp.bfloat16)
        block_tiles = jnp.einsum("rba,rkbc->rkac", own_part.astype(jnp.float32), a_times_p.astype(jnp.float32))
        block_tiles = jnp.where(active_mask[:, :, None, None], block_tiles, jnp.zeros_like(block_tiles)).reshape(ROWS_DEV * KA, BLOCK_ENTRIES)
        segment_index = jnp.where(active_mask, coarse_slot_part, COARSE_BLOCKS).reshape(-1).astype(jnp.int32)
        return grand_total + jax.ops.segment_sum(block_tiles, segment_index, COARSE_BLOCKS + 1), None

    begin_offset = jnp.zeros((COARSE_BLOCKS + 1, BLOCK_ENTRIES), jnp.float32)
    grand_total, _ = lax.scan(accumulate, begin_offset, (a_split, col_split, count_split, slot_split, own_split))
    return grand_total[:COARSE_BLOCKS]
```

```python
import functools

import jax
import jax.numpy as jnp
from jax import lax
from jax.experimental import pallas as pl
from jax.experimental.pallas import tpu as pltpu
from jax.sharding import PartitionSpec as P

BS = 64
LANES = 128
PAIRS = 32
CAP = 4
SLOT_DEV = 8
CAP2 = 4
VMEM_LIMIT = 32 * 1024 * 1024


def lane_of(shape):
    return lax.broadcasted_iota(jnp.int32, shape, len(shape) - 1)


def distinct(keep, owner, local, members, width):
    lanes = lane_of((owner.shape[0], LANES))
    of_owner = jnp.where((lanes == owner) & keep, 1.0, 0.0).astype(jnp.bfloat16)
    of_local = jnp.where(lanes == local, 1.0, 0.0).astype(jnp.bfloat16)
    counts = lax.dot_general(
        of_owner, of_local, (((0,), (0,)), ((), ())), preferred_element_type=jnp.float32
    )[:members]
    present = counts > 0.5
    below = lax.broadcasted_iota(jnp.int32, (LANES, LANES), 0) < lane_of((LANES, LANES))
    rank = jnp.dot(
        jnp.where(present, 1.0, 0.0).astype(jnp.bfloat16),
        jnp.where(below, 1.0, 0.0).astype(jnp.bfloat16),
        preferred_element_type=jnp.float32,
    )
    ranks_of_owner = jnp.dot(
        of_owner[:, :members], rank.astype(jnp.bfloat16), preferred_element_type=jnp.float32
    )
    own_rank = jnp.sum(
        jnp.where(lanes == local, ranks_of_owner, 0.0), axis=1, keepdims=True
    ).astype(jnp.int32)
    return own_rank, present, rank.astype(jnp.int32)


def plan_kernel(members, groups, place_ref, cols_ref, count_ref, slot_ref, p_ref, want_ref, index_ref, pq_ref, stage):
    rows, per_row = cols_ref.shape
    group_at, member_at = place_ref[0], place_ref[1]

    def as_rows(ref):
        return jnp.concatenate([ref[:, k : k + 1] for k in range(per_row)], axis=0)

    cols, slots = as_rows(cols_ref), as_rows(slot_ref)
    live = jnp.concatenate([count_ref[...] > k for k in range(per_row)], axis=0)
    device_of = cols // rows
    local = cols % rows
    col_group = device_of // members
    col_member = device_of % members
    in_group = col_group == group_at
    own = in_group & (col_member == member_at)
    wanted = live & in_group & (col_member != member_at)
    low = col_group == lax.rem(group_at + groups - 1, groups)
    rank, present, ranks = distinct(wanted, col_member, local, members, rows)
    base = members * CAP
    source = jnp.where(
        in_group,
        jnp.where(own, base + local, col_member * CAP + jnp.clip(rank, 0, CAP - 1)),
        jnp.where(low, base + rows + local, base + 2 * rows + local),
    )
    source = jnp.where(live, source, base)

    owner = slots // SLOT_DEV % members
    slot = slots % SLOT_DEV
    slot_rank, slot_present, slot_ranks = distinct(live, owner, slot, members, SLOT_DEV)
    target = jnp.where(live, owner * CAP2 + jnp.clip(slot_rank, 0, CAP2 - 1), members * CAP2)

    lanes = lane_of((members, LANES))
    want = jnp.zeros((members, LANES), jnp.int32)
    for s in range(CAP):
        row = jnp.sum(jnp.where(present & (ranks == s), lanes, 0), axis=1, keepdims=True)
        want = jnp.where(lanes == s, row, want)
    for s in range(CAP2):
        row = jnp.sum(jnp.where(slot_present & (slot_ranks == s), lanes, 0), axis=1, keepdims=True)
        want = jnp.where(lanes == CAP + s, row, want)
    want_ref[...] = want

    lanes = lane_of((rows, LANES))
    index = jnp.zeros((rows, LANES), jnp.int32)
    for k in range(per_row):
        index = jnp.where(lanes == k, source[k * rows : (k + 1) * rows], index)
        index = jnp.where(lanes == per_row + k, target[k * rows : (k + 1) * rows], index)
    index_ref[...] = index

    left = lanes < BS
    for h in range(PAIRS // 2):
        a = p_ref[:, h * LANES : (h + 1) * LANES].astype(jnp.float32)
        b = p_ref[:, (h + PAIRS // 2) * LANES : (h + PAIRS // 2 + 1) * LANES].astype(jnp.float32)
        a_swap, b_swap = pltpu.roll(a, BS, 1), pltpu.roll(b, BS, 1)
        stage[pl.ds(2 * h * rows, rows), :] = jnp.where(left, a, b_swap)
        stage[pl.ds((2 * h + 1) * rows, rows), :] = jnp.where(left, a_swap, b)
    for j in range(rows):
        pq_ref[j] = stage[pl.ds(j, PAIRS, stride=rows), :].astype(jnp.bfloat16)


def pack_kernel(members, asked_ref, pq_ref, out_ref):
    for member in range(members):
        for s in range(CAP):
            out_ref[member * CAP + s] = pq_ref[asked_ref[member, s]]


def tiles_kernel(members, index_ref, a_ref, p_ref, got_ref, pq_ref, low_ref, high_ref, out_ref,
                 table, stage, own_stage, own, total, sem):
    rows, per_row, _ = a_ref.shape
    base = members * CAP
    copies = [
        pltpu.make_async_copy(got_ref, table.at[pl.ds(0, base)], sem.at[0]),
        pltpu.make_async_copy(pq_ref, table.at[pl.ds(base, rows)], sem.at[1]),
        pltpu.make_async_copy(low_ref, table.at[pl.ds(base + rows, rows)], sem.at[2]),
        pltpu.make_async_copy(high_ref, table.at[pl.ds(base + 2 * rows, rows)], sem.at[3]),
    ]
    for copy in copies:
        copy.start()

    row_at = lax.broadcasted_iota(jnp.int32, (LANES, LANES), 0)
    lane_at = lane_of((LANES, LANES))
    col_at = row_at % BS
    order = (row_at // BS) * BS + (col_at % 2) * (BS // 2) + col_at // 2
    shuffle = jnp.where(lane_at == order, 1.0, 0.0).astype(jnp.bfloat16)
    for r in range(PAIRS):
        own_stage[pl.ds(r * rows, rows), :] = jnp.dot(
            p_ref[:, r * LANES : (r + 1) * LANES], shuffle, preferred_element_type=jnp.float32
        )
    for j in range(rows):
        own[j] = own_stage[pl.ds(j, PAIRS, stride=rows), :].astype(jnp.bfloat16)

    def clear(at, carry):
        total[at] = jnp.zeros((PAIRS, LANES), jnp.float32)
        return carry

    lax.fori_loop(0, members * CAP2 + 1, clear, 0, unroll=8)
    for copy in copies:
        copy.wait()

    left = lane_of((PAIRS, LANES)) < BS
    zero = jnp.zeros((PAIRS, LANES), jnp.bfloat16)

    def one(i, carry):
        at = lax.rem(i, 2)
        for r in range(PAIRS):
            stage[at, pl.ds(r * per_row, per_row), :] = a_ref[i, :, r * LANES : (r + 1) * LANES].astype(jnp.float32)
        halves = []
        for k in range(per_row):
            a_pairs = stage[at, pl.ds(k, PAIRS, stride=per_row), :].astype(jnp.bfloat16)
            block = table[index_ref[i, k]]
            swap = jnp.concatenate([block[:, BS:], block[:, :BS]], axis=1)
            both = jnp.concatenate(
                [
                    jnp.where(left, block, zero),
                    jnp.where(left, swap, zero),
                    jnp.where(left, zero, swap),
                    jnp.where(left, zero, block),
                ],
                axis=0,
            )
            halves.append(jnp.dot(a_pairs, both, preferred_element_type=jnp.float32).astype(jnp.bfloat16))
        product = lax.dot_general(
            own[i], jnp.concatenate(halves, axis=1), (((0,), (0,)), ((), ())), preferred_element_type=jnp.float32
        )
        for k in range(per_row):
            part = product[:, k * LANES : (k + 1) * LANES]
            kept = jnp.where(left, part[:PAIRS], part[3 * PAIRS :])
            moved = jnp.where(left, part[PAIRS : 2 * PAIRS], part[2 * PAIRS : 3 * PAIRS])
            to = index_ref[i, per_row + k]
            total[to] += kept + pltpu.roll(moved, BS, 1)
        return carry

    lax.fori_loop(0, rows, one, 0, unroll=2)
    out_ref[...] = total[pl.ds(0, members * CAP2)].astype(jnp.bfloat16)


def sum_kernel(members, asked_ref, got_ref, out_ref, total):
    total[...] = jnp.zeros_like(total)
    for member in range(members):
        for s in range(CAP2):
            to = pl.multiple_of(asked_ref[member, CAP + s] * PAIRS, PAIRS)
            total[pl.ds(to, PAIRS), :] += got_ref[member * CAP2 + s].astype(jnp.float32)
    for r in range(PAIRS):
        out_ref[:, r * LANES : (r + 1) * LANES] = total[pl.ds(r, SLOT_DEV, stride=PAIRS), :]


def body(a_blocks, p_blocks, a_cols, a_count, tile_slot):
    rows, per_row, area = a_blocks.shape
    members = lax.axis_size("row")
    groups = lax.axis_size("grp")
    place = jnp.stack([lax.axis_index("grp"), lax.axis_index("row")]).astype(jnp.int32)
    smem = pl.BlockSpec(memory_space=pltpu.SMEM)
    vmem = pl.BlockSpec(memory_space=pltpu.VMEM)
    anywhere = pl.BlockSpec(memory_space=pl.ANY)
    params = pltpu.CompilerParams(vmem_limit_bytes=VMEM_LIMIT)
    blocks = lambda n: jax.ShapeDtypeStruct((n, PAIRS, LANES), jnp.bfloat16)

    want, index, pq = pl.pallas_call(
        functools.partial(plan_kernel, members, groups),
        out_shape=(
            jax.ShapeDtypeStruct((members, LANES), jnp.int32),
            jax.ShapeDtypeStruct((rows, LANES), jnp.int32),
            blocks(rows),
        ),
        in_specs=[smem, vmem, vmem, vmem, vmem],
        out_specs=(vmem, vmem, vmem),
        scratch_shapes=[pltpu.VMEM((PAIRS * rows, LANES), jnp.float32)],
        compiler_params=params,
        name="plan",
    )(place, a_cols, a_count.reshape(rows, 1), tile_slot, p_blocks)

    forward = [(i, (i + 1) % groups) for i in range(groups)]
    low = lax.ppermute(pq, "grp", forward)
    high = lax.ppermute(pq, "grp", [(target, source) for source, target in forward])

    asked = lax.all_to_all(want.reshape(members, 1, LANES), "row", 0, 0, tiled=True).reshape(members, LANES)
    send = pl.pallas_call(
        functools.partial(pack_kernel, members),
        out_shape=blocks(members * CAP),
        in_specs=[smem, vmem],
        out_specs=vmem,
        compiler_params=params,
        name="pack",
    )(asked, pq)
    got = lax.all_to_all(
        send.reshape(members, CAP, PAIRS, LANES), "row", 0, 0, tiled=True
    ).reshape(members * CAP, PAIRS, LANES)

    sums = pl.pallas_call(
        functools.partial(tiles_kernel, members),
        out_shape=blocks(members * CAP2),
        in_specs=[smem, vmem, vmem, anywhere, anywhere, anywhere, anywhere],
        out_specs=vmem,
        scratch_shapes=[
            pltpu.VMEM((members * CAP + 3 * rows, PAIRS, LANES), jnp.bfloat16),
            pltpu.VMEM((2, PAIRS * per_row, LANES), jnp.float32),
            pltpu.VMEM((PAIRS * rows, LANES), jnp.float32),
            pltpu.VMEM((rows, PAIRS, LANES), jnp.bfloat16),
            pltpu.VMEM((members * CAP2 + 1, PAIRS, LANES), jnp.float32),
            pltpu.SemaphoreType.DMA((4,)),
        ],
        compiler_params=params,
        name="tiles",
    )(index, a_blocks, p_blocks, got, pq, low, high)
    parts = lax.all_to_all(
        sums.reshape(members, CAP2, PAIRS, LANES), "row", 0, 0, tiled=True
    ).reshape(members * CAP2, PAIRS, LANES)

    return pl.pallas_call(
        functools.partial(sum_kernel, members),
        out_shape=jax.ShapeDtypeStruct((SLOT_DEV, area), jnp.float32),
        in_specs=[smem, vmem],
        out_specs=vmem,
        scratch_shapes=[pltpu.VMEM((SLOT_DEV * PAIRS, LANES), jnp.float32)],
        compiler_params=params,
        name="holders",
    )(asked, parts)


def solution(mesh):
    placed = (
        P(("grp", "row"), None, None),
        P(("grp", "row"), None),
        P(("grp", "row"), None),
        P(("grp", "row")),
        P(("grp", "row"), None),
    )
    return jax.shard_map(
        body, mesh=mesh, in_specs=placed, out_specs=P(("grp", "row"), None), check_vma=False
    )
```

```python
import functools

import jax
import jax.numpy as jnp
from jax import lax
from jax.experimental import pallas as pl
from jax.experimental.pallas import tpu as pltpu
from jax.sharding import PartitionSpec as P

BS = 64
LANES = 128
PAIRS = 32
CAP = 4
SLOT_DEV = 8
CAP2 = 4
GROUP = 16
VMEM_LIMIT = 12 * 1024 * 1024
WIDE_LIMIT = 40 * 1024 * 1024
SPARE = 1664
BF16 = jnp.bfloat16
F32 = jnp.float32


def lane_of(shape):
    return lax.broadcasted_iota(jnp.int32, shape, len(shape) - 1)


def row_of(shape):
    return lax.broadcasted_iota(jnp.int32, shape, len(shape) - 2)


def ones(mask):
    return jnp.where(mask, 1.0, 0.0).astype(BF16)


def dot(a, b, contract):
    return lax.dot_general(a, b, ((contract[:1], contract[1:]), ((), ())), preferred_element_type=F32)


def table_of(owner, local, keep, members, width):
    per_row, rows = owner.shape
    counts = jnp.zeros((members, width), F32)
    for k in range(per_row):
        of_owner = ones((row_of((members, rows)) == owner[k : k + 1]) & keep[k : k + 1])
        of_local = ones(row_of((width, rows)) == local[k : k + 1])
        counts += dot(of_owner, of_local, (1, 1))
    present = counts > 0.5
    before = ones(row_of((width, width)) < lane_of((width, width)))
    return present, dot(ones(present), before, (1, 0))


def rank_of(owner, local, rank):
    per_row, rows = owner.shape
    members, width = rank.shape
    result = jnp.zeros((per_row, rows), jnp.int32)
    for k in range(per_row):
        of_owner = ones(row_of((members, rows)) == owner[k : k + 1])
        ranks = dot(rank.astype(BF16), of_owner, (0, 0))
        mine = jnp.sum(jnp.where(row_of((width, rows)) == local[k : k + 1], ranks, 0.0), axis=0, keepdims=True)
        result = jnp.where(row_of((per_row, rows)) == k, mine.astype(jnp.int32), result)
    return result


def chosen(present, rank, cap, first, result):
    members, width = present.shape
    ids, lanes = lane_of((members, width)), lane_of((members, LANES))
    for s in range(cap):
        one = jnp.sum(jnp.where(present & (rank == float(s)), ids, 0), axis=1, keepdims=True)
        result = jnp.where(lanes == first + s, one, result)
    return result


def split_cols(cols, rows, members):
    device_of = cols // rows
    return cols % rows, device_of // members, device_of % members


def read_entries(entry_ref):
    per_row, rows = SLOT_DEV, entry_ref.shape[1]
    cols, slots, count = (entry_ref[n * per_row : (n + 1) * per_row, :] for n in range(3))
    return cols, slots, row_of((per_row, rows)) < count, per_row, rows


def plan_kernel(members, place_ref, entry_ref, want_ref):
    cols, slots, live, per_row, rows = read_entries(entry_ref)
    local, group, member = split_cols(cols, rows, members)
    wanted = live & (group == place_ref[0]) & (member != place_ref[1])
    present, rank = table_of(member, local, wanted, members, rows)
    want = chosen(present, rank, CAP, 0, jnp.zeros((members, LANES), jnp.int32))
    present, rank = table_of(slots // SLOT_DEV % members, slots % SLOT_DEV, live, members, SLOT_DEV)
    want_ref[...] = chosen(present, rank, CAP2, CAP, want)


def lists_kernel(members, groups, place_ref, entry_ref, lists_ref):
    cols, slots, live, per_row, rows = read_entries(entry_ref)
    entries = per_row * rows
    local, group, member = split_cols(cols, rows, members)
    at_k = row_of((per_row, rows))
    in_group = group == place_ref[0]
    far = in_group & (member != place_ref[1])
    _, rank = table_of(member, local, live & far, members, rows)
    far_source = member * CAP + jnp.clip(rank_of(member, local, rank), 0, CAP - 1)
    low = group == lax.rem(place_ref[0] + groups - 1, groups)
    near_source = jnp.where(in_group, local, jnp.where(low, rows + local, 2 * rows + local))
    source = jnp.where(far, far_source, near_source)

    owner, slot = slots // SLOT_DEV % members, slots % SLOT_DEV
    _, rank = table_of(owner, slot, live, members, SLOT_DEV)
    target = owner * CAP2 + jnp.clip(rank_of(owner, slot, rank), 0, CAP2 - 1)

    entry = lane_of((per_row, rows)) * per_row + at_k
    before = ones(row_of((rows, rows)) < lane_of((rows, rows)))
    above = ones(lane_of((per_row, per_row)) < row_of((per_row, per_row)))
    result = jnp.zeros((SLOT_DEV, entries), jnp.int32)
    for which, mask in enumerate((live & ~far, live & far)):
        inside = dot(ones(mask), before, (1, 0))
        totals = jnp.sum(jnp.where(mask, 1.0, 0.0), axis=1, keepdims=True)
        earlier = dot(above, jnp.broadcast_to(totals, (per_row, LANES)).astype(BF16), (1, 0))[:, :1]
        at = jnp.where(mask, (inside + earlier).astype(jnp.int32), -1)
        count = jnp.sum(totals, axis=0, keepdims=True).astype(jnp.int32)
        placed = jnp.zeros((SLOT_DEV, entries), F32)
        for k in range(per_row):
            here = ones(row_of((entries, rows)) == at[k : k + 1])
            kind = row_of((SLOT_DEV, rows))
            value = jnp.where(kind == 0, entry[k : k + 1], jnp.where(kind == 1, source[k : k + 1], target[k : k + 1]))
            placed += dot(value.astype(F32).astype(BF16), here, (1, 1))
        placed = placed.astype(jnp.int32)
        code = placed[:1] * 65536 + placed[1:2] * 256 + placed[2:3]
        lanes = lane_of((1, entries))
        code = jnp.where(lanes < count, code, members * CAP2)
        kind = row_of((SLOT_DEV, entries))
        result = jnp.where(kind == which, code, result)
        result = jnp.where(kind == 2 + which, count, result)
    lists_ref[...] = result


def prepare_kernel(p_ref, pq_ref, stage):
    rows = p_ref.shape[0]
    left = lane_of((rows, LANES)) < BS
    for h in range(PAIRS // 2):
        a = p_ref[:, h * LANES : (h + 1) * LANES].astype(F32)
        b = p_ref[:, (h + PAIRS // 2) * LANES : (h + PAIRS // 2 + 1) * LANES].astype(F32)
        stage[pl.ds(2 * h * rows, rows), :] = jnp.where(left, a, pltpu.roll(b, BS, 1))
        stage[pl.ds((2 * h + 1) * rows, rows), :] = jnp.where(left, pltpu.roll(a, BS, 1), b)
    for j in range(rows):
        pq_ref[j] = stage[pl.ds(j, PAIRS, stride=rows), :].astype(BF16)


def relay(a_ref, p_ref, pairs_ref, own_ref, stage, own_stage):
    rows, per_row, _ = a_ref.shape
    row_at, lane_at = row_of((LANES, LANES)), lane_of((LANES, LANES))
    col_at = row_at % BS
    order = (col_at % 2) * BS + (row_at // BS) * (BS // 2) + col_at // 2
    shuffle = ones(lane_at == order)
    for r in range(PAIRS):
        own_stage[pl.ds(r * rows, rows), :] = jnp.dot(
            p_ref[:, r * LANES : (r + 1) * LANES], shuffle, preferred_element_type=F32
        )
    at_once = LANES // PAIRS
    for first in range(0, rows, at_once):
        turned = jnp.concatenate(
            [own_stage[pl.ds(first + j, PAIRS, stride=rows), :] for j in range(at_once)], axis=0
        ).T
        for j in range(at_once):
            mine = turned[:, j * PAIRS : (j + 1) * PAIRS]
            own_ref[first + j] = jnp.concatenate(
                [mine[n * PAIRS : (n + 1) * PAIRS] for n in range(at_once)], axis=1
            ).astype(BF16)

    def one(i, carry):
        at = lax.rem(i, 2)
        for r in range(PAIRS):
            stage[at, pl.ds(r * per_row, per_row), :] = a_ref[i, :, r * LANES : (r + 1) * LANES].astype(F32)
        for k in range(per_row):
            pairs_ref[i * per_row + k] = stage[at, pl.ds(k, PAIRS, stride=per_row), :].astype(BF16)
        return carry

    lax.fori_loop(0, rows, one, 0, unroll=2)


def twice(block):
    left, zero = lane_of(block.shape) < BS, jnp.zeros(block.shape, block.dtype)
    swap = jnp.concatenate([block[:, BS:], block[:, :BS]], axis=1)
    parts = [
        jnp.where(left, block, zero),
        jnp.where(left, swap, zero),
        jnp.where(left, zero, swap),
        jnp.where(left, zero, block),
    ]
    return jnp.concatenate(parts, axis=0)


def add_tiles(lists_ref, which, group, per_row, table_ref, pairs_ref, own_ref, total_ref):
    def one(step, carry):
        codes = [lists_ref[which, step * group + n] for n in range(group)]
        rights = [twice(table_ref[(code >> 8) & 255]) for code in codes]
        halves = [
            jnp.dot(pairs_ref[code >> 16], right, preferred_element_type=F32).astype(BF16)
            for code, right in zip(codes, rights)
        ]
        rights = [twice(half) for half in halves]
        tiles = [
            jnp.dot(own_ref[(code >> 16) // per_row], right, preferred_element_type=F32)
            for code, right in zip(codes, rights)
        ]
        for code, tile in zip(codes, tiles):
            total_ref[code & 255] += tile
        return carry

    lax.fori_loop(0, (lists_ref[2 + which, 0] + group - 1) // group, one, 0)


def views(work_ref, entries, per_row):
    return work_ref.at[pl.ds(0, entries)], work_ref.at[pl.ds(entries, entries // per_row)]


def clear(total_ref):
    def one(at, carry):
        total_ref[at] = jnp.zeros((PAIRS, LANES), F32)
        return carry

    lax.fori_loop(0, total_ref.shape[0], one, 0, unroll=8)


def near_kernel(per_row, lists_ref, a_ref, p_ref, pq_ref, low_ref, high_ref, work_ref, near_ref,
                table, stage, own_stage, total_ref, sem):
    pairs_ref, own_ref = views(work_ref, lists_ref.shape[1], per_row)
    relay(a_ref, p_ref, pairs_ref, own_ref, stage, own_stage)
    rows = pq_ref.shape[0]
    for at, ref in enumerate((pq_ref, low_ref, high_ref)):
        table[pl.ds(at * rows, rows)] = ref[...]
    clear(total_ref)
    add_tiles(lists_ref, 0, GROUP, per_row, table, pairs_ref, own_ref, total_ref)
    sums = total_ref.shape[0] - 1
    copy = pltpu.make_async_copy(total_ref.at[pl.ds(0, sums)], near_ref.at[pl.ds(0, sums)], sem)
    copy.start()
    copy.wait()


def far_kernel(per_row, lists_ref, work_ref, got_ref, near_ref, out_ref, total, near, sem):
    copy = pltpu.make_async_copy(near_ref.at[pl.ds(0, near.shape[0])], near, sem)
    copy.start()
    pairs_ref, own_ref = views(work_ref, lists_ref.shape[1], per_row)
    clear(total)
    add_tiles(lists_ref, 1, GROUP, per_row, got_ref, pairs_ref, own_ref, total)
    copy.wait()

    def one(at, carry):
        out_ref[at] = (total[at] + near[at]).astype(BF16)
        return carry

    lax.fori_loop(0, out_ref.shape[0], one, 0, unroll=8)


def pack_kernel(members, asked_ref, pq_ref, out_ref):
    for member in range(members):
        for s in range(CAP):
            out_ref[member * CAP + s] = pq_ref[asked_ref[member, s]]


def sum_kernel(members, asked_ref, got_ref, out_ref, *totals):
    for total in totals:
        total[...] = jnp.zeros_like(total)
    for member in range(members):
        for s, total in enumerate(totals):
            to = pl.multiple_of(asked_ref[member, CAP + s] * PAIRS, PAIRS)
            total[pl.ds(to, PAIRS), :] += got_ref[member * CAP2 + s].astype(F32)
    for r in range(PAIRS):
        out_ref[:, r * LANES : (r + 1) * LANES] = sum(
            total[pl.ds(r, SLOT_DEV, stride=PAIRS), :] for total in totals
        )


def body(a_blocks, p_blocks, a_cols, a_count, tile_slot):
    rows, per_row, area = a_blocks.shape
    members = lax.axis_size("row")
    groups = lax.axis_size("grp")
    entries = rows * per_row
    place = jnp.stack([lax.axis_index("grp"), lax.axis_index("row")]).astype(jnp.int32)
    smem = pl.BlockSpec(memory_space=pltpu.SMEM)
    vmem = pl.BlockSpec(memory_space=pltpu.VMEM)
    hbm = pl.BlockSpec(memory_space=pltpu.HBM)
    blocks = lambda n, dtype=BF16: jax.ShapeDtypeStruct((n, PAIRS, LANES), dtype)
    ints = lambda *shape: jax.ShapeDtypeStruct(shape, jnp.int32)

    def call(kernel, name, ins, outs, scratch, us, out_specs=vmem, limit=VMEM_LIMIT):
        return pl.pallas_call(
            kernel,
            out_shape=outs,
            in_specs=ins,
            out_specs=out_specs,
            scratch_shapes=scratch,
            compiler_params=pltpu.CompilerParams(vmem_limit_bytes=limit),
            cost_estimate=pl.CostEstimate(flops=0, bytes_accessed=int(us * 3e6), transcendentals=0),
            name=name,
        )

    entry = jnp.concatenate(
        [a_cols.T, tile_slot.T, jnp.broadcast_to(a_count[None], (per_row, rows))], axis=0
    )
    want = call(
        functools.partial(plan_kernel, members), "plan", [smem, vmem], ints(members, LANES), [], 2
    )(place, entry)
    asked = lax.all_to_all(want.reshape(members, 1, LANES), "row", 0, 0, tiled=True).reshape(members, LANES)

    pq = call(
        prepare_kernel, "prepare", [vmem], blocks(rows), [pltpu.VMEM((PAIRS * rows, LANES), F32)], 0.1
    )(p_blocks)
    forward = [(i, (i + 1) % groups) for i in range(groups)]
    low = lax.ppermute(pq, "grp", forward)
    high = lax.ppermute(pq, "grp", [(target, source) for source, target in forward])

    send = call(
        functools.partial(pack_kernel, members), "pack", [smem, vmem], blocks(members * CAP), [], 2
    )(asked, pq)
    got = lax.all_to_all(
        send.reshape(members, CAP, PAIRS, LANES), "row", 0, 0, tiled=True
    ).reshape(members * CAP, PAIRS, LANES)

    lists = call(
        functools.partial(lists_kernel, members, groups),
        "lists",
        [smem, vmem],
        ints(SLOT_DEV, entries),
        [],
        0.1,
    )(place, entry)
    work, near = call(
        functools.partial(near_kernel, per_row),
        "near",
        [smem, vmem, vmem, vmem, vmem, vmem],
        (blocks(entries + rows), blocks(SPARE, F32)),
        [
            pltpu.VMEM((3 * rows, PAIRS, LANES), BF16),
            pltpu.VMEM((2, PAIRS * per_row, LANES), F32),
            pltpu.VMEM((PAIRS * rows, LANES), F32),
            pltpu.VMEM((members * CAP2 + 1, PAIRS, LANES), F32),
            pltpu.SemaphoreType.DMA,
        ],
        0.1,
        (vmem, hbm),
        WIDE_LIMIT,
    )(lists, a_blocks, p_blocks, pq, low, high)
    sums = call(
        functools.partial(far_kernel, per_row),
        "far",
        [smem, vmem, vmem, hbm],
        blocks(members * CAP2),
        [
            pltpu.VMEM((members * CAP2 + 1, PAIRS, LANES), F32),
            pltpu.VMEM((members * CAP2, PAIRS, LANES), F32),
            pltpu.SemaphoreType.DMA,
        ],
        6,
        limit=WIDE_LIMIT,
    )(lists, work, got, near)
    parts = lax.all_to_all(
        sums.reshape(members, CAP2, PAIRS, LANES), "row", 0, 0, tiled=True
    ).reshape(members * CAP2, PAIRS, LANES)

    return call(
        functools.partial(sum_kernel, members),
        "holders",
        [smem, vmem],
        jax.ShapeDtypeStruct((SLOT_DEV, area), F32),
        [pltpu.VMEM((SLOT_DEV * PAIRS, LANES), F32)] * CAP2,
        2,
    )(asked, parts)


def solution(mesh):
    placed = (
        P(("grp", "row"), None, None),
        P(("grp", "row"), None),
        P(("grp", "row"), None),
        P(("grp", "row")),
        P(("grp", "row"), None),
    )
    return jax.shard_map(
        body, mesh=mesh, in_specs=placed, out_specs=P(("grp", "row"), None), check_vma=False
    )
```

```python
import functools

import jax
import jax.numpy as jnp
from jax import lax
from jax.experimental import pallas as pl
from jax.experimental.pallas import tpu as pltpu
from jax.sharding import PartitionSpec as P

BS = 64
LANES = 128
PAIRS = 32
CAP = 4
SLOT_DEV = 8
CAP2 = 4
STEPS = (64, 32)
QUARTERS = 4
VMEM_LIMIT = 12 * 1024 * 1024
WIDE_LIMIT = 40 * 1024 * 1024
PLAN_LIMIT = 60 * 1024 * 1024
SPARE = 1664
BF16 = jnp.bfloat16
F32 = jnp.float32


def lane_of(shape):
    return lax.broadcasted_iota(jnp.int32, shape, len(shape) - 1)


def row_of(shape):
    return lax.broadcasted_iota(jnp.int32, shape, len(shape) - 2)


def ones(mask):
    return jnp.where(mask, 1.0, 0.0).astype(BF16)


def dot(a, b, contract):
    return lax.dot_general(a, b, ((contract[:1], contract[1:]), ((), ())), preferred_element_type=F32)


def table_of(owner, local, keep, members, width):
    per_row, rows = owner.shape
    counts = jnp.zeros((members, width), F32)
    for k in range(per_row):
        of_owner = ones((row_of((members, rows)) == owner[k : k + 1]) & keep[k : k + 1])
        of_local = ones(row_of((width, rows)) == local[k : k + 1])
        counts += dot(of_owner, of_local, (1, 1))
    present = counts > 0.5
    before = ones(row_of((width, width)) < lane_of((width, width)))
    return present, dot(ones(present), before, (1, 0))


def rank_of(owner, local, rank):
    per_row, rows = owner.shape
    members, width = rank.shape
    result = jnp.zeros((per_row, rows), jnp.int32)
    for k in range(per_row):
        of_owner = ones(row_of((members, rows)) == owner[k : k + 1])
        ranks = dot(rank.astype(BF16), of_owner, (0, 0))
        mine = jnp.sum(jnp.where(row_of((width, rows)) == local[k : k + 1], ranks, 0.0), axis=0, keepdims=True)
        result = jnp.where(row_of((per_row, rows)) == k, mine.astype(jnp.int32), result)
    return result


def chosen(present, rank, cap, first, result):
    members, width = present.shape
    ids, lanes = lane_of((members, width)), lane_of((members, LANES))
    for s in range(cap):
        one = jnp.sum(jnp.where(present & (rank == float(s)), ids, 0), axis=1, keepdims=True)
        result = jnp.where(lanes == first + s, one, result)
    return result


def split_cols(cols, rows, members):
    device_of = cols // rows
    return cols % rows, device_of // members, device_of % members


def plan_kernel(members, cols_ref, count_ref, slot_ref, want_ref):
    per_row, rows = cols_ref.shape
    local, group, member = split_cols(cols_ref[...], rows, members)
    live = row_of((per_row, rows)) < count_ref[...]
    slots = slot_ref[...]
    wanted = live & (group == lax.axis_index("grp")) & (member != lax.axis_index("row"))
    present, rank = table_of(member, local, wanted, members, rows)
    want = chosen(present, rank, CAP, 0, jnp.zeros((members, LANES), jnp.int32))
    present, rank = table_of(slots // SLOT_DEV % members, slots % SLOT_DEV, live, members, SLOT_DEV)
    want_ref[...] = chosen(present, rank, CAP2, CAP, want)


def lists_kernel(members, groups, cols_ref, count_ref, slot_ref, asked_ref, lists_ref, spread_ref):
    places = members * CAP2 * QUARTERS
    from_member = ones(row_of((members, places)) == lane_of((members, places)) // (CAP2 * QUARTERS))
    names = asked_ref[...][:, :SLOT_DEV].astype(F32).astype(BF16)
    named = dot(names, from_member, (0, 0))
    at = lane_of((SLOT_DEV, places))
    mine = row_of((SLOT_DEV, places)) == CAP + at // QUARTERS % CAP2
    slot_at = jnp.sum(jnp.where(mine, named, 0.0), axis=0, keepdims=True).astype(jnp.int32)
    at, to = lane_of((QUARTERS * SLOT_DEV, places)), row_of((QUARTERS * SLOT_DEV, places))
    spread_ref[...] = ones((to % SLOT_DEV == slot_at) & (to // SLOT_DEV == at % QUARTERS))

    per_row, rows = cols_ref.shape
    entries = per_row * rows
    at_k = row_of((per_row, rows))
    local, group, member = split_cols(cols_ref[...], rows, members)
    live = at_k < count_ref[...]
    slots = slot_ref[...]
    group_at = lax.axis_index("grp")
    in_group = group == group_at
    far = in_group & (member != lax.axis_index("row"))
    _, rank = table_of(member, local, live & far, members, rows)
    far_source = member * CAP + jnp.clip(rank_of(member, local, rank), 0, CAP - 1)
    low = group == lax.rem(group_at + groups - 1, groups)
    near_source = jnp.where(in_group, local, jnp.where(low, rows + local, 2 * rows + local))
    source = jnp.where(far, far_source, near_source)

    owner, slot = slots // SLOT_DEV % members, slots % SLOT_DEV
    _, rank = table_of(owner, slot, live, members, SLOT_DEV)
    target = owner * CAP2 + jnp.clip(rank_of(owner, slot, rank), 0, CAP2 - 1)

    entry = lane_of((per_row, rows)) * per_row + at_k
    before = ones(row_of((rows, rows)) < lane_of((rows, rows)))
    above = ones(lane_of((per_row, per_row)) < row_of((per_row, per_row)))
    result = jnp.zeros((SLOT_DEV, entries), jnp.int32)
    for which, mask in enumerate((live & ~far, live & far)):
        inside = dot(ones(mask), before, (1, 0))
        totals = jnp.sum(jnp.where(mask, 1.0, 0.0), axis=1, keepdims=True)
        earlier = dot(above, jnp.broadcast_to(totals, (per_row, LANES)).astype(BF16), (1, 0))[:, :1]
        at = jnp.where(mask, (inside + earlier).astype(jnp.int32), -1)
        count = jnp.sum(totals, axis=0, keepdims=True).astype(jnp.int32)
        placed = jnp.zeros((SLOT_DEV, entries), F32)
        for k in range(per_row):
            here = ones(row_of((entries, rows)) == at[k : k + 1])
            kind = row_of((SLOT_DEV, rows))
            value = jnp.where(kind == 0, entry[k : k + 1], jnp.where(kind == 1, source[k : k + 1], target[k : k + 1]))
            placed += dot(value.astype(F32).astype(BF16), here, (1, 1))
        placed = placed.astype(jnp.int32)
        code = placed[:1] * 65536 + placed[1:2] * 256 + placed[2:3]
        lanes = lane_of((1, entries))
        code = jnp.where(lanes < count, code, members * CAP2)
        kind = row_of((SLOT_DEV, entries))
        result = jnp.where(kind == which, code, result)
        result = jnp.where(kind == 2 + which, count, result)
    lists_ref[...] = result


def prepare_kernel(p_ref, pq_ref, stage):
    rows = p_ref.shape[0]
    left = lane_of((rows, LANES)) < BS
    for h in range(PAIRS // 2):
        a = p_ref[:, h * LANES : (h + 1) * LANES].astype(F32)
        b = p_ref[:, (h + PAIRS // 2) * LANES : (h + PAIRS // 2 + 1) * LANES].astype(F32)
        stage[pl.ds(2 * h * rows, rows), :] = jnp.where(left, a, pltpu.roll(b, BS, 1))
        stage[pl.ds((2 * h + 1) * rows, rows), :] = jnp.where(left, pltpu.roll(a, BS, 1), b)
    for j in range(rows):
        pq_ref[j] = stage[pl.ds(j, PAIRS, stride=rows), :].astype(BF16)


def relay(a_ref, p_ref, pairs_ref, own_ref, stage, own_stage):
    rows, per_row, _ = a_ref.shape
    row_at, lane_at = row_of((LANES, LANES)), lane_of((LANES, LANES))
    col_at = row_at % BS
    order = (col_at % 2) * BS + (row_at // BS) * (BS // 2) + col_at // 2
    shuffle = ones(lane_at == order)
    for r in range(PAIRS):
        own_stage[pl.ds(r * rows, rows), :] = jnp.dot(
            p_ref[:, r * LANES : (r + 1) * LANES], shuffle, preferred_element_type=F32
        )
    at_once = LANES // PAIRS
    for first in range(0, rows, at_once):
        turned = jnp.concatenate(
            [own_stage[pl.ds(first + j, PAIRS, stride=rows), :] for j in range(at_once)], axis=0
        ).T
        for j in range(at_once):
            mine = turned[:, j * PAIRS : (j + 1) * PAIRS]
            own_ref[first + j] = jnp.concatenate(
                [mine[n * PAIRS : (n + 1) * PAIRS] for n in range(at_once)], axis=1
            ).astype(BF16)

    def one(i, carry):
        at = lax.rem(i, 2)
        for r in range(PAIRS):
            stage[at, pl.ds(r * per_row, per_row), :] = a_ref[i, :, r * LANES : (r + 1) * LANES].astype(F32)
        for k in range(per_row):
            pairs_ref[i * per_row + k] = stage[at, pl.ds(k, PAIRS, stride=per_row), :].astype(BF16)
        return carry

    lax.fori_loop(0, rows, one, 0, unroll=2)


def twice(block):
    left, zero = lane_of(block.shape) < BS, jnp.zeros(block.shape, block.dtype)
    swap = jnp.concatenate([block[:, BS:], block[:, :BS]], axis=1)
    parts = [
        jnp.where(left, block, zero),
        jnp.where(left, swap, zero),
        jnp.where(left, zero, swap),
        jnp.where(left, zero, block),
    ]
    return jnp.concatenate(parts, axis=0)


def two_products(lefts, rights):
    both = jnp.dot(
        jnp.concatenate(lefts, axis=0), jnp.concatenate(rights, axis=1), preferred_element_type=F32
    )
    return [both[:PAIRS, :LANES], both[PAIRS:, LANES:]]


def add_tiles(codes_ref, count, per_row, table_ref, pairs_ref, own_ref, total_ref):
    def step(start, group):
        codes = [codes_ref[start + n] for n in range(group)]
        halves, tiles = [], []
        for n in range(0, group, 2):
            rights = [twice(table_ref[(code >> 8) & 255]) for code in codes[n : n + 2]]
            halves += two_products([pairs_ref[code >> 16] for code in codes[n : n + 2]], rights)
        for n in range(0, group, 2):
            rights = [twice(half.astype(BF16)) for half in halves[n : n + 2]]
            tiles += two_products([own_ref[(code >> 16) // per_row] for code in codes[n : n + 2]], rights)
        for code, tile in zip(codes, tiles):
            total_ref[code & 255] += tile

    large, small = STEPS
    whole = (count + large - 1 - small) // large
    rest = jnp.maximum(count - whole * large, 0)

    def one_large(n, carry):
        step(n * large, large)
        return carry

    def one_small(n, carry):
        step(whole * large + n * small, small)
        return carry

    lax.fori_loop(0, whole, one_large, 0)
    lax.fori_loop(0, (rest + small - 1) // small, one_small, 0)


def views(work_ref, entries, per_row):
    return work_ref.at[pl.ds(0, entries)], work_ref.at[pl.ds(entries, entries // per_row)]


def clear(total_ref):
    def one(at, carry):
        total_ref[at] = jnp.zeros((PAIRS, LANES), F32)
        return carry

    lax.fori_loop(0, total_ref.shape[0], one, 0, unroll=8)


def near_kernel(per_row, lists_ref, a_ref, p_ref, pq_ref, low_ref, high_ref, work_ref, near_ref,
                table, stage, own_stage, total_ref, sem):
    pairs_ref, own_ref = views(work_ref, lists_ref.shape[1], per_row)
    relay(a_ref, p_ref, pairs_ref, own_ref, stage, own_stage)
    rows = pq_ref.shape[0]
    for at, ref in enumerate((pq_ref, low_ref, high_ref)):
        table[pl.ds(at * rows, rows)] = ref[...]
    clear(total_ref)
    add_tiles(lists_ref.at[0], lists_ref[2, 0], per_row, table, pairs_ref, own_ref, total_ref)
    sums = total_ref.shape[0] - 1
    copy = pltpu.make_async_copy(total_ref.at[pl.ds(0, sums)], near_ref.at[pl.ds(0, sums)], sem)
    copy.start()
    copy.wait()


def far_kernel(per_row, lists_from, work_ref, got_ref, near_ref, out_ref, total, lists_ref, sem):
    blocks = total.shape[0] - 1
    copies = [
        pltpu.make_async_copy(near_ref.at[pl.ds(0, blocks)], total.at[pl.ds(0, blocks)], sem.at[0]),
        pltpu.make_async_copy(lists_from, lists_ref, sem.at[1]),
    ]
    for copy in copies:
        copy.start()
    total[blocks] = jnp.zeros((PAIRS, LANES), F32)
    pairs_ref, own_ref = views(work_ref, lists_ref.shape[1], per_row)
    for copy in copies:
        copy.wait()
    add_tiles(lists_ref.at[1], lists_ref[3, 0], per_row, got_ref, pairs_ref, own_ref, total)
    for member in range(out_ref.shape[0]):
        for at in range(PAIRS // QUARTERS):
            rows = total.at[pl.ds(member * CAP2, CAP2)].reshape(CAP2 * PAIRS, LANES)[
                pl.ds(at, CAP2 * QUARTERS, stride=PAIRS // QUARTERS), :
            ]
            out_ref[member, :, at * LANES : (at + 1) * LANES] = rows.astype(BF16)


def pack_kernel(members, asked_ref, pq_ref, out_ref):
    for member in range(members):
        for s in range(CAP):
            out_ref[member * CAP + s] = pq_ref[asked_ref[member, s]]


def sum_kernel(spread_ref, got_ref, out_ref):
    result = jnp.dot(spread_ref[...], got_ref[...], preferred_element_type=F32)
    width = got_ref.shape[1]
    for n in range(QUARTERS):
        out_ref[:, n * width : (n + 1) * width] = result[n * SLOT_DEV : (n + 1) * SLOT_DEV]


def body(a_blocks, p_blocks, a_cols, a_count, tile_slot):
    rows, per_row, area = a_blocks.shape
    members = lax.axis_size("row")
    groups = lax.axis_size("grp")
    entries = rows * per_row
    smem = pl.BlockSpec(memory_space=pltpu.SMEM)
    vmem = pl.BlockSpec(memory_space=pltpu.VMEM)
    hbm = pl.BlockSpec(memory_space=pltpu.HBM)
    blocks = lambda n, dtype=BF16: jax.ShapeDtypeStruct((n, PAIRS, LANES), dtype)
    ints = lambda *shape: jax.ShapeDtypeStruct(shape, jnp.int32)

    def call(kernel, name, ins, outs, scratch, us, out_specs=vmem, limit=VMEM_LIMIT):
        return pl.pallas_call(
            kernel,
            out_shape=outs,
            in_specs=ins,
            out_specs=out_specs,
            scratch_shapes=scratch,
            compiler_params=pltpu.CompilerParams(vmem_limit_bytes=limit),
            cost_estimate=pl.CostEstimate(flops=0, bytes_accessed=int(us * 3e6), transcendentals=0),
            name=name,
        )

    entry = (a_cols.T, a_count.reshape(1, rows), tile_slot.T)
    want = call(
        functools.partial(plan_kernel, members), "plan", [vmem] * 3, ints(members, LANES), [], 2, limit=PLAN_LIMIT
    )(*entry)
    asked = lax.all_to_all(want.reshape(members, 1, LANES), "row", 0, 0, tiled=True).reshape(members, LANES)

    pq = call(
        prepare_kernel, "prepare", [vmem], blocks(rows), [pltpu.VMEM((PAIRS * rows, LANES), F32)], 0.1
    )(p_blocks)
    forward = [(i, (i + 1) % groups) for i in range(groups)]
    low = lax.ppermute(pq, "grp", forward)
    high = lax.ppermute(pq, "grp", [(target, source) for source, target in forward])

    send = call(
        functools.partial(pack_kernel, members), "pack", [smem, vmem], blocks(members * CAP), [], 2
    )(asked, pq)
    got = lax.all_to_all(
        send.reshape(members, CAP, PAIRS, LANES), "row", 0, 0, tiled=True
    ).reshape(members * CAP, PAIRS, LANES)

    lists, spread = call(
        functools.partial(lists_kernel, members, groups),
        "lists",
        [vmem] * 4,
        (ints(SLOT_DEV, entries), jax.ShapeDtypeStruct((QUARTERS * SLOT_DEV, members * CAP2 * QUARTERS), BF16)),
        [],
        0.1,
        (vmem, vmem),
    )(*entry, asked)
    work, near = call(
        functools.partial(near_kernel, per_row),
        "near",
        [smem, vmem, vmem, vmem, vmem, vmem],
        (blocks(entries + rows), blocks(SPARE, F32)),
        [
            pltpu.VMEM((3 * rows, PAIRS, LANES), BF16),
            pltpu.VMEM((2, PAIRS * per_row, LANES), F32),
            pltpu.VMEM((PAIRS * rows, LANES), F32),
            pltpu.VMEM((members * CAP2 + 1, PAIRS, LANES), F32),
            pltpu.SemaphoreType.DMA,
        ],
        0.1,
        (vmem, hbm),
        WIDE_LIMIT,
    )(lists, a_blocks, p_blocks, pq, low, high)
    sums = call(
        functools.partial(far_kernel, per_row),
        "far",
        [vmem, vmem, vmem, hbm],
        jax.ShapeDtypeStruct((members, CAP2 * QUARTERS, area // QUARTERS), BF16),
        [
            pltpu.VMEM((members * CAP2 + 1, PAIRS, LANES), F32),
            pltpu.SMEM((SLOT_DEV, entries), jnp.int32),
            pltpu.SemaphoreType.DMA((2,)),
        ],
        6,
        limit=WIDE_LIMIT,
    )(lists, work, got, near)
    parts = lax.all_to_all(sums, "row", 0, 0, tiled=True).reshape(-1, area // QUARTERS)

    return call(
        sum_kernel, "holders", [vmem, vmem], jax.ShapeDtypeStruct((SLOT_DEV, area), F32), [], 2
    )(spread, parts)


def solution(mesh):
    placed = (
        P(("grp", "row"), None, None),
        P(("grp", "row"), None),
        P(("grp", "row"), None),
        P(("grp", "row")),
        P(("grp", "row"), None),
    )
    return jax.shard_map(
        body, mesh=mesh, in_specs=placed, out_specs=P(("grp", "row"), None), check_vma=False
    )
```

```python
import functools

import jax
import jax.numpy as jnp
from jax import lax
from jax.experimental import pallas as pl
from jax.experimental.pallas import tpu as pltpu
from jax.sharding import PartitionSpec as P

BS = 64
LANES = 128
PAIRS = 32
CAP = 4
SLOT_DEV = 8
CAP2 = 4
STEPS = (64, 32)
ASK, ROWS, SUMS = (tuple(reversed(range(32))),) * 3
QUARTERS = 4
VMEM_LIMIT = 12 * 1024 * 1024
WIDE_LIMIT = 40 * 1024 * 1024
PLAN_LIMIT = 60 * 1024 * 1024
SPARE = 1664
BF16 = jnp.bfloat16
F32 = jnp.float32


def lane_of(shape):
    return lax.broadcasted_iota(jnp.int32, shape, len(shape) - 1)


def row_of(shape):
    return lax.broadcasted_iota(jnp.int32, shape, len(shape) - 2)


def ones(mask):
    return jnp.where(mask, 1.0, 0.0).astype(BF16)


def dot(a, b, contract):
    return lax.dot_general(a, b, ((contract[:1], contract[1:]), ((), ())), preferred_element_type=F32)


def table_of(owner, local, keep, members, width):
    per_row, rows = owner.shape
    counts = jnp.zeros((members, width), F32)
    for k in range(per_row):
        of_owner = ones((row_of((members, rows)) == owner[k : k + 1]) & keep[k : k + 1])
        of_local = ones(row_of((width, rows)) == local[k : k + 1])
        counts += dot(of_owner, of_local, (1, 1))
    present = counts > 0.5
    before = ones(row_of((width, width)) < lane_of((width, width)))
    return present, dot(ones(present), before, (1, 0))


def rank_of(owner, local, rank):
    per_row, rows = owner.shape
    members, width = rank.shape
    result = jnp.zeros((per_row, rows), jnp.int32)
    for k in range(per_row):
        of_owner = ones(row_of((members, rows)) == owner[k : k + 1])
        ranks = dot(rank.astype(BF16), of_owner, (0, 0))
        mine = jnp.sum(jnp.where(row_of((width, rows)) == local[k : k + 1], ranks, 0.0), axis=0, keepdims=True)
        result = jnp.where(row_of((per_row, rows)) == k, mine.astype(jnp.int32), result)
    return result


def chosen(present, rank, cap, first, result):
    members, width = present.shape
    ids, lanes = lane_of((members, width)), lane_of((members, LANES))
    for s in range(cap):
        one = jnp.sum(jnp.where(present & (rank == float(s)), ids, 0), axis=1, keepdims=True)
        result = jnp.where(lanes == first + s, one, result)
    return result


def place_in(order, member):
    result = jnp.zeros_like(member)
    for at, who in enumerate(order):
        result = jnp.where(member == who, at, result)
    return result


def exchange(x, order):
    return lax.all_to_all(x, "row", 0, 0, tiled=True, axis_index_groups=[list(order)])


def split_cols(cols, rows, members):
    device_of = cols // rows
    return cols % rows, device_of // members, device_of % members


def plan_kernel(members, cols_ref, count_ref, slot_ref, want_ref):
    per_row, rows = cols_ref.shape
    local, group, member = split_cols(cols_ref[...], rows, members)
    live = row_of((per_row, rows)) < count_ref[...]
    slots = slot_ref[...]
    wanted = live & (group == lax.axis_index("grp")) & (member != lax.axis_index("row"))
    present, rank = table_of(place_in(ASK, member), local, wanted, members, rows)
    want = chosen(present, rank, CAP, 0, jnp.zeros((members, LANES), jnp.int32))
    holder = place_in(ASK, slots // SLOT_DEV % members)
    present, rank = table_of(holder, slots % SLOT_DEV, live, members, SLOT_DEV)
    want_ref[...] = chosen(present, rank, CAP2, CAP, want)


def lists_kernel(members, groups, cols_ref, count_ref, slot_ref, asked_ref, lists_ref, spread_ref):
    places = members * CAP2 * QUARTERS
    sender = lane_of((members, places)) // (CAP2 * QUARTERS)
    from_member = jnp.zeros((members, places), jnp.bool_)
    for at, who in enumerate(SUMS):
        from_member = from_member | ((sender == at) & (row_of((members, places)) == ASK.index(who)))
    from_member = ones(from_member)
    names = asked_ref[...][:, :SLOT_DEV].astype(F32).astype(BF16)
    named = dot(names, from_member, (0, 0))
    at = lane_of((SLOT_DEV, places))
    mine = row_of((SLOT_DEV, places)) == CAP + at // QUARTERS % CAP2
    slot_at = jnp.sum(jnp.where(mine, named, 0.0), axis=0, keepdims=True).astype(jnp.int32)
    at, to = lane_of((QUARTERS * SLOT_DEV, places)), row_of((QUARTERS * SLOT_DEV, places))
    spread_ref[...] = ones((to % SLOT_DEV == slot_at) & (to // SLOT_DEV == at % QUARTERS))

    per_row, rows = cols_ref.shape
    entries = per_row * rows
    at_k = row_of((per_row, rows))
    local, group, member = split_cols(cols_ref[...], rows, members)
    live = at_k < count_ref[...]
    slots = slot_ref[...]
    group_at = lax.axis_index("grp")
    in_group = group == group_at
    far = in_group & (member != lax.axis_index("row"))
    _, rank = table_of(member, local, live & far, members, rows)
    far_source = place_in(ROWS, member) * CAP + jnp.clip(rank_of(member, local, rank), 0, CAP - 1)
    low = group == lax.rem(group_at + groups - 1, groups)
    near_source = jnp.where(in_group, local, jnp.where(low, rows + local, 2 * rows + local))
    source = jnp.where(far, far_source, near_source)

    owner, slot = slots // SLOT_DEV % members, slots % SLOT_DEV
    _, rank = table_of(owner, slot, live, members, SLOT_DEV)
    target = place_in(SUMS, owner) * CAP2 + jnp.clip(rank_of(owner, slot, rank), 0, CAP2 - 1)

    entry = lane_of((per_row, rows)) * per_row + at_k
    before = ones(row_of((rows, rows)) < lane_of((rows, rows)))
    above = ones(lane_of((per_row, per_row)) < row_of((per_row, per_row)))
    result = jnp.zeros((SLOT_DEV, entries), jnp.int32)
    for which, mask in enumerate((live & ~far, live & far)):
        inside = dot(ones(mask), before, (1, 0))
        totals = jnp.sum(jnp.where(mask, 1.0, 0.0), axis=1, keepdims=True)
        earlier = dot(above, jnp.broadcast_to(totals, (per_row, LANES)).astype(BF16), (1, 0))[:, :1]
        at = jnp.where(mask, (inside + earlier).astype(jnp.int32), -1)
        count = jnp.sum(totals, axis=0, keepdims=True).astype(jnp.int32)
        placed = jnp.zeros((SLOT_DEV, entries), F32)
        for k in range(per_row):
            here = ones(row_of((entries, rows)) == at[k : k + 1])
            kind = row_of((SLOT_DEV, rows))
            value = jnp.where(kind == 0, entry[k : k + 1], jnp.where(kind == 1, source[k : k + 1], target[k : k + 1]))
            placed += dot(value.astype(F32).astype(BF16), here, (1, 1))
        placed = placed.astype(jnp.int32)
        code = placed[:1] * 65536 + placed[1:2] * 256 + placed[2:3]
        lanes = lane_of((1, entries))
        code = jnp.where(lanes < count, code, members * CAP2)
        kind = row_of((SLOT_DEV, entries))
        result = jnp.where(kind == which, code, result)
        result = jnp.where(kind == 2 + which, count, result)
    lists_ref[...] = result


def prepare_kernel(p_ref, pq_ref, stage):
    rows = p_ref.shape[0]
    left = lane_of((rows, LANES)) < BS
    for h in range(PAIRS // 2):
        a = p_ref[:, h * LANES : (h + 1) * LANES].astype(F32)
        b = p_ref[:, (h + PAIRS // 2) * LANES : (h + PAIRS // 2 + 1) * LANES].astype(F32)
        stage[pl.ds(2 * h * rows, rows), :] = jnp.where(left, a, pltpu.roll(b, BS, 1))
        stage[pl.ds((2 * h + 1) * rows, rows), :] = jnp.where(left, pltpu.roll(a, BS, 1), b)
    for j in range(rows):
        pq_ref[j] = stage[pl.ds(j, PAIRS, stride=rows), :].astype(BF16)


def relay(a_ref, p_ref, pairs_ref, own_ref, stage, own_stage):
    rows, per_row, _ = a_ref.shape
    row_at, lane_at = row_of((LANES, LANES)), lane_of((LANES, LANES))
    col_at = row_at % BS
    order = (col_at % 2) * BS + (row_at // BS) * (BS // 2) + col_at // 2
    shuffle = ones(lane_at == order)
    for r in range(PAIRS):
        own_stage[pl.ds(r * rows, rows), :] = jnp.dot(
            p_ref[:, r * LANES : (r + 1) * LANES], shuffle, preferred_element_type=F32
        )
    at_once = LANES // PAIRS
    for first in range(0, rows, at_once):
        turned = jnp.concatenate(
            [own_stage[pl.ds(first + j, PAIRS, stride=rows), :] for j in range(at_once)], axis=0
        ).T
        for j in range(at_once):
            mine = turned[:, j * PAIRS : (j + 1) * PAIRS]
            own_ref[first + j] = jnp.concatenate(
                [mine[n * PAIRS : (n + 1) * PAIRS] for n in range(at_once)], axis=1
            ).astype(BF16)

    def one(i, carry):
        at = lax.rem(i, 2)
        for r in range(PAIRS):
            stage[at, pl.ds(r * per_row, per_row), :] = a_ref[i, :, r * LANES : (r + 1) * LANES].astype(F32)
        for k in range(per_row):
            pairs_ref[i * per_row + k] = stage[at, pl.ds(k, PAIRS, stride=per_row), :].astype(BF16)
        return carry

    lax.fori_loop(0, rows, one, 0, unroll=2)


def twice(block):
    left, zero = lane_of(block.shape) < BS, jnp.zeros(block.shape, block.dtype)
    swap = jnp.concatenate([block[:, BS:], block[:, :BS]], axis=1)
    parts = [
        jnp.where(left, block, zero),
        jnp.where(left, swap, zero),
        jnp.where(left, zero, swap),
        jnp.where(left, zero, block),
    ]
    return jnp.concatenate(parts, axis=0)


def two_products(lefts, rights):
    both = jnp.dot(
        jnp.concatenate(lefts, axis=0), jnp.concatenate(rights, axis=1), preferred_element_type=F32
    )
    return [both[:PAIRS, :LANES], both[PAIRS:, LANES:]]


def add_tiles(codes_ref, count, per_row, table_ref, pairs_ref, own_ref, total_ref):
    def step(start, group):
        codes = [codes_ref[start + n] for n in range(group)]
        halves, tiles = [], []
        for n in range(0, group, 2):
            rights = [twice(table_ref[(code >> 8) & 255]) for code in codes[n : n + 2]]
            halves += two_products([pairs_ref[code >> 16] for code in codes[n : n + 2]], rights)
        for n in range(0, group, 2):
            rights = [twice(half.astype(BF16)) for half in halves[n : n + 2]]
            tiles += two_products([own_ref[(code >> 16) // per_row] for code in codes[n : n + 2]], rights)
        for code, tile in zip(codes, tiles):
            total_ref[code & 255] += tile

    large, small = STEPS
    whole = (count + large - 1 - small) // large
    rest = jnp.maximum(count - whole * large, 0)

    def one_large(n, carry):
        step(n * large, large)
        return carry

    def one_small(n, carry):
        step(whole * large + n * small, small)
        return carry

    lax.fori_loop(0, whole, one_large, 0)
    lax.fori_loop(0, (rest + small - 1) // small, one_small, 0)


def views(work_ref, entries, per_row):
    return work_ref.at[pl.ds(0, entries)], work_ref.at[pl.ds(entries, entries // per_row)]


def clear(total_ref):
    def one(at, carry):
        total_ref[at] = jnp.zeros((PAIRS, LANES), F32)
        return carry

    lax.fori_loop(0, total_ref.shape[0], one, 0, unroll=8)


def near_kernel(per_row, lists_ref, a_ref, p_ref, pq_ref, low_ref, high_ref, work_ref, near_ref,
                table, stage, own_stage, total_ref, sem):
    pairs_ref, own_ref = views(work_ref, lists_ref.shape[1], per_row)
    relay(a_ref, p_ref, pairs_ref, own_ref, stage, own_stage)
    rows = pq_ref.shape[0]
    for at, ref in enumerate((pq_ref, low_ref, high_ref)):
        table[pl.ds(at * rows, rows)] = ref[...]
    clear(total_ref)
    add_tiles(lists_ref.at[0], lists_ref[2, 0], per_row, table, pairs_ref, own_ref, total_ref)
    sums = total_ref.shape[0] - 1
    copy = pltpu.make_async_copy(total_ref.at[pl.ds(0, sums)], near_ref.at[pl.ds(0, sums)], sem)
    copy.start()
    copy.wait()


def far_kernel(per_row, lists_from, work_ref, got_ref, near_ref, out_ref, total, lists_ref, sem):
    blocks = total.shape[0] - 1
    copies = [
        pltpu.make_async_copy(near_ref.at[pl.ds(0, blocks)], total.at[pl.ds(0, blocks)], sem.at[0]),
        pltpu.make_async_copy(lists_from, lists_ref, sem.at[1]),
    ]
    for copy in copies:
        copy.start()
    total[blocks] = jnp.zeros((PAIRS, LANES), F32)
    pairs_ref, own_ref = views(work_ref, lists_ref.shape[1], per_row)
    for copy in copies:
        copy.wait()
    add_tiles(lists_ref.at[1], lists_ref[3, 0], per_row, got_ref, pairs_ref, own_ref, total)
    for member in range(out_ref.shape[0]):
        for at in range(PAIRS // QUARTERS):
            rows = total.at[pl.ds(member * CAP2, CAP2)].reshape(CAP2 * PAIRS, LANES)[
                pl.ds(at, CAP2 * QUARTERS, stride=PAIRS // QUARTERS), :
            ]
            out_ref[member, :, at * LANES : (at + 1) * LANES] = rows.astype(BF16)


def pack_kernel(members, asked_ref, pq_ref, out_ref):
    for at in range(members):
        for s in range(CAP):
            out_ref[at * CAP + s] = pq_ref[asked_ref[ASK.index(ROWS[at]), s]]


def sum_kernel(spread_ref, got_ref, out_ref):
    result = jnp.dot(spread_ref[...], got_ref[...], preferred_element_type=F32)
    width = got_ref.shape[1]
    for n in range(QUARTERS):
        out_ref[:, n * width : (n + 1) * width] = result[n * SLOT_DEV : (n + 1) * SLOT_DEV]


def body(a_blocks, p_blocks, a_cols, a_count, tile_slot):
    rows, per_row, area = a_blocks.shape
    members = lax.axis_size("row")
    groups = lax.axis_size("grp")
    entries = rows * per_row
    smem = pl.BlockSpec(memory_space=pltpu.SMEM)
    vmem = pl.BlockSpec(memory_space=pltpu.VMEM)
    hbm = pl.BlockSpec(memory_space=pltpu.HBM)
    blocks = lambda n, dtype=BF16: jax.ShapeDtypeStruct((n, PAIRS, LANES), dtype)
    ints = lambda *shape: jax.ShapeDtypeStruct(shape, jnp.int32)

    def call(kernel, name, ins, outs, scratch, us, out_specs=vmem, limit=VMEM_LIMIT):
        return pl.pallas_call(
            kernel,
            out_shape=outs,
            in_specs=ins,
            out_specs=out_specs,
            scratch_shapes=scratch,
            compiler_params=pltpu.CompilerParams(vmem_limit_bytes=limit),
            cost_estimate=pl.CostEstimate(flops=0, bytes_accessed=int(us * 3e6), transcendentals=0),
            name=name,
        )

    entry = (a_cols.T, a_count.reshape(1, rows), tile_slot.T)
    want = call(
        functools.partial(plan_kernel, members), "plan", [vmem] * 3, ints(members, LANES), [], 2, limit=PLAN_LIMIT
    )(*entry)
    asked = exchange(want.reshape(members, 1, LANES), ASK).reshape(members, LANES)

    pq = call(
        prepare_kernel, "prepare", [vmem], blocks(rows), [pltpu.VMEM((PAIRS * rows, LANES), F32)], 0.1
    )(p_blocks)
    forward = [(i, (i + 1) % groups) for i in range(groups)]
    low = lax.ppermute(pq, "grp", forward)
    high = lax.ppermute(pq, "grp", [(target, source) for source, target in forward])

    send = call(
        functools.partial(pack_kernel, members), "pack", [smem, vmem], blocks(members * CAP), [], 2
    )(asked, pq)
    got = exchange(send.reshape(members, CAP, PAIRS, LANES), ROWS).reshape(members * CAP, PAIRS, LANES)

    lists, spread = call(
        functools.partial(lists_kernel, members, groups),
        "lists",
        [vmem] * 4,
        (ints(SLOT_DEV, entries), jax.ShapeDtypeStruct((QUARTERS * SLOT_DEV, members * CAP2 * QUARTERS), BF16)),
        [],
        0.1,
        (vmem, vmem),
    )(*entry, asked)
    work, near = call(
        functools.partial(near_kernel, per_row),
        "near",
        [smem, vmem, vmem, vmem, vmem, vmem],
        (blocks(entries + rows), blocks(SPARE, F32)),
        [
            pltpu.VMEM((3 * rows, PAIRS, LANES), BF16),
            pltpu.VMEM((2, PAIRS * per_row, LANES), F32),
            pltpu.VMEM((PAIRS * rows, LANES), F32),
            pltpu.VMEM((members * CAP2 + 1, PAIRS, LANES), F32),
            pltpu.SemaphoreType.DMA,
        ],
        0.1,
        (vmem, hbm),
        WIDE_LIMIT,
    )(lists, a_blocks, p_blocks, pq, low, high)
    sums = call(
        functools.partial(far_kernel, per_row),
        "far",
        [vmem, vmem, vmem, hbm],
        jax.ShapeDtypeStruct((members, CAP2 * QUARTERS, area // QUARTERS), BF16),
        [
            pltpu.VMEM((members * CAP2 + 1, PAIRS, LANES), F32),
            pltpu.SMEM((SLOT_DEV, entries), jnp.int32),
            pltpu.SemaphoreType.DMA((2,)),
        ],
        6,
        limit=WIDE_LIMIT,
    )(lists, work, got, near)
    parts = exchange(sums, SUMS).reshape(-1, area // QUARTERS)

    return call(
        sum_kernel, "holders", [vmem, vmem], jax.ShapeDtypeStruct((SLOT_DEV, area), F32), [], 2
    )(spread, parts)


def solution(mesh):
    placed = (
        P(("grp", "row"), None, None),
        P(("grp", "row"), None),
        P(("grp", "row"), None),
        P(("grp", "row")),
        P(("grp", "row"), None),
    )
    return jax.shard_map(
        body, mesh=mesh, in_specs=placed, out_specs=P(("grp", "row"), None), check_vma=False
    )
```

```python
import functools

import jax
import jax.numpy as jnp
from jax import lax
from jax.experimental import pallas as pl
from jax.experimental.pallas import tpu as pltpu
from jax.sharding import PartitionSpec as P

BS = 64
LANES = 128
PAIRS = 32
CAP = 4
SLOT_DEV = 8
CAP2 = 4
COUNTS = 6
STEPS = (64, 32)
ASK, ROWS, SUMS = (tuple(reversed(range(32))),) * 3
QUARTERS = 4
VMEM_LIMIT = 12 * 1024 * 1024
WIDE_LIMIT = 40 * 1024 * 1024
PLAN_LIMIT = 60 * 1024 * 1024
SPARE = 1664
BF16 = jnp.bfloat16
F32 = jnp.float32


def lane_of(shape):
    return lax.broadcasted_iota(jnp.int32, shape, len(shape) - 1)


def row_of(shape):
    return lax.broadcasted_iota(jnp.int32, shape, len(shape) - 2)


def ones(mask):
    return jnp.where(mask, 1.0, 0.0).astype(BF16)


def dot(a, b, contract):
    return lax.dot_general(a, b, ((contract[:1], contract[1:]), ((), ())), preferred_element_type=F32)


def table_of(owner, local, keep, members, width):
    per_row, rows = owner.shape
    counts = jnp.zeros((members, width), F32)
    for k in range(per_row):
        of_owner = ones((row_of((members, rows)) == owner[k : k + 1]) & keep[k : k + 1])
        of_local = ones(row_of((width, rows)) == local[k : k + 1])
        counts += dot(of_owner, of_local, (1, 1))
    present = counts > 0.5
    before = ones(row_of((width, width)) < lane_of((width, width)))
    return present, dot(ones(present), before, (1, 0))


def rank_of(owner, local, rank):
    per_row, rows = owner.shape
    members, width = rank.shape
    result = jnp.zeros((per_row, rows), jnp.int32)
    for k in range(per_row):
        of_owner = ones(row_of((members, rows)) == owner[k : k + 1])
        ranks = dot(rank.astype(BF16), of_owner, (0, 0))
        mine = jnp.sum(jnp.where(row_of((width, rows)) == local[k : k + 1], ranks, 0.0), axis=0, keepdims=True)
        result = jnp.where(row_of((per_row, rows)) == k, mine.astype(jnp.int32), result)
    return result


def chosen(present, rank, cap, first, result):
    members, width = present.shape
    ids, lanes = lane_of((members, width)), lane_of((members, LANES))
    for s in range(cap):
        one = jnp.sum(jnp.where(present & (rank == float(s)), ids, 0), axis=1, keepdims=True)
        result = jnp.where(lanes == first + s, one, result)
    return result


def place_in(order, member):
    result = jnp.zeros_like(member)
    for at, who in enumerate(order):
        result = jnp.where(member == who, at, result)
    return result


def exchange(x, order):
    return lax.all_to_all(x, "row", 0, 0, tiled=True, axis_index_groups=[list(order)])


def split_cols(cols, rows, members):
    device_of = cols // rows
    return cols % rows, device_of // members, device_of % members


def plan_kernel(members, cols_ref, count_ref, slot_ref, want_ref):
    per_row, rows = cols_ref.shape
    local, group, member = split_cols(cols_ref[...], rows, members)
    live = row_of((per_row, rows)) < count_ref[...]
    slots = slot_ref[...]
    wanted = live & (group == lax.axis_index("grp")) & (member != lax.axis_index("row"))
    present, rank = table_of(place_in(ASK, member), local, wanted, members, rows)
    want = chosen(present, rank, CAP, 0, jnp.zeros((members, LANES), jnp.int32))
    holder = place_in(ASK, slots // SLOT_DEV % members)
    present, rank = table_of(holder, slots % SLOT_DEV, live, members, SLOT_DEV)
    want_ref[...] = chosen(present, rank, CAP2, CAP, want)


def lists_kernel(members, groups, cols_ref, count_ref, slot_ref, asked_ref, lists_ref, spread_ref):
    places = members * CAP2 * QUARTERS
    sender = lane_of((members, places)) // (CAP2 * QUARTERS)
    from_member = jnp.zeros((members, places), jnp.bool_)
    for at, who in enumerate(SUMS):
        from_member = from_member | ((sender == at) & (row_of((members, places)) == ASK.index(who)))
    from_member = ones(from_member)
    names = asked_ref[...][:, :SLOT_DEV].astype(F32).astype(BF16)
    named = dot(names, from_member, (0, 0))
    at = lane_of((SLOT_DEV, places))
    mine = row_of((SLOT_DEV, places)) == CAP + at // QUARTERS % CAP2
    slot_at = jnp.sum(jnp.where(mine, named, 0.0), axis=0, keepdims=True).astype(jnp.int32)
    at, to = lane_of((QUARTERS * SLOT_DEV, places)), row_of((QUARTERS * SLOT_DEV, places))
    spread_ref[...] = ones((to % SLOT_DEV == slot_at) & (to // SLOT_DEV == at % QUARTERS))

    per_row, rows = cols_ref.shape
    entries = per_row * rows
    at_k = row_of((per_row, rows))
    local, group, member = split_cols(cols_ref[...], rows, members)
    live = at_k < count_ref[...]
    slots = slot_ref[...]
    group_at = lax.axis_index("grp")
    in_group = group == group_at
    far = in_group & (member != lax.axis_index("row"))
    _, rank = table_of(member, local, live & far, members, rows)
    far_source = place_in(ROWS, member) * CAP + jnp.clip(rank_of(member, local, rank), 0, CAP - 1)
    low = group == lax.rem(group_at + groups - 1, groups)
    near_source = jnp.where(in_group, local, jnp.where(low, rows + local, 2 * rows + local))
    source = jnp.where(far, far_source, near_source)

    owner, slot = slots // SLOT_DEV % members, slots % SLOT_DEV
    _, rank = table_of(owner, slot, live, members, SLOT_DEV)
    target = place_in(SUMS, owner) * CAP2 + jnp.clip(rank_of(owner, slot, rank), 0, CAP2 - 1)

    entry = lane_of((per_row, rows)) * per_row + at_k
    before = ones(row_of((rows, rows)) < lane_of((rows, rows)))
    above = ones(lane_of((per_row, per_row)) < row_of((per_row, per_row)))
    halves = entries // LANES
    result = jnp.zeros((SLOT_DEV, LANES), jnp.int32)
    for which, mask in enumerate((live & ~far, live & far)):
        inside = dot(ones(mask), before, (1, 0))
        totals = jnp.sum(jnp.where(mask, 1.0, 0.0), axis=1, keepdims=True)
        earlier = dot(above, jnp.broadcast_to(totals, (per_row, LANES)).astype(BF16), (1, 0))[:, :1]
        at = jnp.where(mask, (inside + earlier).astype(jnp.int32), -1)
        count = jnp.sum(totals, axis=0, keepdims=True).astype(jnp.int32)
        placed = jnp.zeros((SLOT_DEV, entries), F32)
        for k in range(per_row):
            here = ones(row_of((entries, rows)) == at[k : k + 1])
            kind = row_of((SLOT_DEV, rows))
            value = jnp.where(kind == 0, entry[k : k + 1], jnp.where(kind == 1, source[k : k + 1], target[k : k + 1]))
            placed += dot(value.astype(F32).astype(BF16), here, (1, 1))
        placed = placed.astype(jnp.int32)
        code = placed[:1] * 65536 + placed[1:2] * 256 + placed[2:3]
        lanes = lane_of((1, entries))
        code = jnp.where(lanes < count, code, members * CAP2)
        kind = row_of((SLOT_DEV, LANES))
        for half in range(halves):
            part = code[:, half * LANES : (half + 1) * LANES]
            result = jnp.where(kind == which * halves + half, part, result)
        result = jnp.where(kind == COUNTS + which, count, result)
    lists_ref[...] = result


def prepare_kernel(p_ref, pq_ref, stage):
    rows = p_ref.shape[0]
    left = lane_of((rows, LANES)) < BS
    for h in range(PAIRS // 2):
        a = p_ref[:, h * LANES : (h + 1) * LANES].astype(F32)
        b = p_ref[:, (h + PAIRS // 2) * LANES : (h + PAIRS // 2 + 1) * LANES].astype(F32)
        stage[pl.ds(2 * h * rows, rows), :] = jnp.where(left, a, pltpu.roll(b, BS, 1))
        stage[pl.ds((2 * h + 1) * rows, rows), :] = jnp.where(left, pltpu.roll(a, BS, 1), b)
    for j in range(rows):
        pq_ref[j] = stage[pl.ds(j, PAIRS, stride=rows), :].astype(BF16)


def relay(a_ref, p_ref, pairs_ref, own_ref, stage, own_stage):
    rows, per_row, _ = a_ref.shape
    row_at, lane_at = row_of((LANES, LANES)), lane_of((LANES, LANES))
    col_at = row_at % BS
    order = (col_at % 2) * BS + (row_at // BS) * (BS // 2) + col_at // 2
    shuffle = ones(lane_at == order)
    for r in range(PAIRS):
        own_stage[pl.ds(r * rows, rows), :] = jnp.dot(
            p_ref[:, r * LANES : (r + 1) * LANES], shuffle, preferred_element_type=F32
        )
    at_once = LANES // PAIRS
    for first in range(0, rows, at_once):
        turned = jnp.concatenate(
            [own_stage[pl.ds(first + j, PAIRS, stride=rows), :] for j in range(at_once)], axis=0
        ).T
        for j in range(at_once):
            mine = turned[:, j * PAIRS : (j + 1) * PAIRS]
            own_ref[first + j] = jnp.concatenate(
                [mine[n * PAIRS : (n + 1) * PAIRS] for n in range(at_once)], axis=1
            ).astype(BF16)

    def one(i, carry):
        at = lax.rem(i, 2)
        for r in range(PAIRS):
            stage[at, pl.ds(r * per_row, per_row), :] = a_ref[i, :, r * LANES : (r + 1) * LANES].astype(F32)
        for k in range(per_row):
            pairs_ref[i * per_row + k] = stage[at, pl.ds(k, PAIRS, stride=per_row), :].astype(BF16)
        return carry

    lax.fori_loop(0, rows, one, 0, unroll=2)


def twice(block):
    left, zero = lane_of(block.shape) < BS, jnp.zeros(block.shape, block.dtype)
    swap = jnp.concatenate([block[:, BS:], block[:, :BS]], axis=1)
    parts = [
        jnp.where(left, block, zero),
        jnp.where(left, swap, zero),
        jnp.where(left, zero, swap),
        jnp.where(left, zero, block),
    ]
    return jnp.concatenate(parts, axis=0)


def two_products(lefts, rights):
    both = jnp.dot(
        jnp.concatenate(lefts, axis=0), jnp.concatenate(rights, axis=1), preferred_element_type=F32
    )
    return [both[:PAIRS, :LANES], both[PAIRS:, LANES:]]


def add_tiles(lists_ref, which, per_row, table_ref, pairs_ref, own_ref, total_ref):
    count = lists_ref[COUNTS + which, 0]
    first = which * (pairs_ref.shape[0] // LANES)

    def step(start, group):
        row, lane = first + start // LANES, lax.rem(start, LANES)
        codes = [lists_ref[row, lane + n] for n in range(group)]
        halves, tiles = [], []
        for n in range(0, group, 2):
            rights = [twice(table_ref[(code >> 8) & 255]) for code in codes[n : n + 2]]
            halves += two_products([pairs_ref[code >> 16] for code in codes[n : n + 2]], rights)
        for n in range(0, group, 2):
            rights = [twice(half.astype(BF16)) for half in halves[n : n + 2]]
            tiles += two_products([own_ref[(code >> 16) // per_row] for code in codes[n : n + 2]], rights)
        for code, tile in zip(codes, tiles):
            total_ref[code & 255] += tile

    large, small = STEPS
    whole = (count + large - 1 - small) // large
    rest = jnp.maximum(count - whole * large, 0)

    def one_large(n, carry):
        step(n * large, large)
        return carry

    def one_small(n, carry):
        step(whole * large + n * small, small)
        return carry

    lax.fori_loop(0, whole, one_large, 0)
    lax.fori_loop(0, (rest + small - 1) // small, one_small, 0)


def views(work_ref, per_row):
    entries = work_ref.shape[0] // (per_row + 1) * per_row
    return work_ref.at[pl.ds(0, entries)], work_ref.at[pl.ds(entries, entries // per_row)]


def clear(total_ref):
    def one(at, carry):
        total_ref[at] = jnp.zeros((PAIRS, LANES), F32)
        return carry

    lax.fori_loop(0, total_ref.shape[0], one, 0, unroll=8)


def near_kernel(per_row, lists_ref, a_ref, p_ref, pq_ref, low_ref, high_ref, work_ref, near_ref,
                table, stage, own_stage, total_ref, sem):
    pairs_ref, own_ref = views(work_ref, per_row)
    relay(a_ref, p_ref, pairs_ref, own_ref, stage, own_stage)
    rows = pq_ref.shape[0]
    for at, ref in enumerate((pq_ref, low_ref, high_ref)):
        table[pl.ds(at * rows, rows)] = ref[...]
    clear(total_ref)
    add_tiles(lists_ref, 0, per_row, table, pairs_ref, own_ref, total_ref)
    sums = total_ref.shape[0] - 1
    copy = pltpu.make_async_copy(total_ref.at[pl.ds(0, sums)], near_ref.at[pl.ds(0, sums)], sem)
    copy.start()
    copy.wait()


def far_kernel(per_row, lists_from, work_ref, got_ref, near_ref, out_ref, total, lists_ref, sem):
    blocks = total.shape[0] - 1
    copies = [
        pltpu.make_async_copy(near_ref.at[pl.ds(0, blocks)], total.at[pl.ds(0, blocks)], sem.at[0]),
        pltpu.make_async_copy(lists_from, lists_ref, sem.at[1]),
    ]
    for copy in copies:
        copy.start()
    total[blocks] = jnp.zeros((PAIRS, LANES), F32)
    pairs_ref, own_ref = views(work_ref, per_row)
    for copy in copies:
        copy.wait()
    add_tiles(lists_ref, 1, per_row, got_ref, pairs_ref, own_ref, total)
    for member in range(out_ref.shape[0]):
        for at in range(PAIRS // QUARTERS):
            rows = total.at[pl.ds(member * CAP2, CAP2)].reshape(CAP2 * PAIRS, LANES)[
                pl.ds(at, CAP2 * QUARTERS, stride=PAIRS // QUARTERS), :
            ]
            out_ref[member, :, at * LANES : (at + 1) * LANES] = rows.astype(BF16)


def pack_kernel(members, asked_ref, pq_ref, out_ref):
    for at in range(members):
        for s in range(CAP):
            out_ref[at * CAP + s] = pq_ref[asked_ref[ASK.index(ROWS[at]), s]]


def sum_kernel(spread_ref, got_ref, out_ref):
    result = jnp.dot(spread_ref[...], got_ref[...], preferred_element_type=F32)
    width = got_ref.shape[1]
    for n in range(QUARTERS):
        out_ref[:, n * width : (n + 1) * width] = result[n * SLOT_DEV : (n + 1) * SLOT_DEV]


def body(a_blocks, p_blocks, a_cols, a_count, tile_slot):
    rows, per_row, area = a_blocks.shape
    members = lax.axis_size("row")
    groups = lax.axis_size("grp")
    entries = rows * per_row
    smem = pl.BlockSpec(memory_space=pltpu.SMEM)
    vmem = pl.BlockSpec(memory_space=pltpu.VMEM)
    hbm = pl.BlockSpec(memory_space=pltpu.HBM)
    blocks = lambda n, dtype=BF16: jax.ShapeDtypeStruct((n, PAIRS, LANES), dtype)
    ints = lambda *shape: jax.ShapeDtypeStruct(shape, jnp.int32)

    def call(kernel, name, ins, outs, scratch, us, out_specs=vmem, limit=VMEM_LIMIT):
        return pl.pallas_call(
            kernel,
            out_shape=outs,
            in_specs=ins,
            out_specs=out_specs,
            scratch_shapes=scratch,
            compiler_params=pltpu.CompilerParams(vmem_limit_bytes=limit),
            cost_estimate=pl.CostEstimate(flops=0, bytes_accessed=int(us * 3e6), transcendentals=0),
            name=name,
        )

    entry = (a_cols.T, a_count.reshape(1, rows), tile_slot.T)
    want = call(
        functools.partial(plan_kernel, members), "plan", [vmem] * 3, ints(members, LANES), [], 2, limit=PLAN_LIMIT
    )(*entry)
    asked = exchange(want.reshape(members, 1, LANES), ASK).reshape(members, LANES)

    pq = call(
        prepare_kernel, "prepare", [vmem], blocks(rows), [pltpu.VMEM((PAIRS * rows, LANES), F32)], 0.1
    )(p_blocks)
    forward = [(i, (i + 1) % groups) for i in range(groups)]
    low = lax.ppermute(pq, "grp", forward)
    high = lax.ppermute(pq, "grp", [(target, source) for source, target in forward])

    send = call(
        functools.partial(pack_kernel, members), "pack", [smem, vmem], blocks(members * CAP), [], 2
    )(asked, pq)
    got = exchange(send.reshape(members, CAP, PAIRS, LANES), ROWS).reshape(members * CAP, PAIRS, LANES)

    lists, spread = call(
        functools.partial(lists_kernel, members, groups),
        "lists",
        [vmem] * 4,
        (ints(SLOT_DEV, LANES), jax.ShapeDtypeStruct((QUARTERS * SLOT_DEV, members * CAP2 * QUARTERS), BF16)),
        [],
        0.1,
        (vmem, vmem),
    )(*entry, asked)
    work, near = call(
        functools.partial(near_kernel, per_row),
        "near",
        [smem, vmem, vmem, vmem, vmem, vmem],
        (blocks(entries + rows), blocks(SPARE, F32)),
        [
            pltpu.VMEM((3 * rows, PAIRS, LANES), BF16),
            pltpu.VMEM((2, PAIRS * per_row, LANES), F32),
            pltpu.VMEM((PAIRS * rows, LANES), F32),
            pltpu.VMEM((members * CAP2 + 1, PAIRS, LANES), F32),
            pltpu.SemaphoreType.DMA,
        ],
        0.1,
        (vmem, hbm),
        WIDE_LIMIT,
    )(lists, a_blocks, p_blocks, pq, low, high)
    sums = call(
        functools.partial(far_kernel, per_row),
        "far",
        [vmem, vmem, vmem, hbm],
        jax.ShapeDtypeStruct((members, CAP2 * QUARTERS, area // QUARTERS), BF16),
        [
            pltpu.VMEM((members * CAP2 + 1, PAIRS, LANES), F32),
            pltpu.SMEM((SLOT_DEV, LANES), jnp.int32),
            pltpu.SemaphoreType.DMA((2,)),
        ],
        6,
        limit=WIDE_LIMIT,
    )(lists, work, got, near)
    parts = exchange(sums, SUMS).reshape(-1, area // QUARTERS)

    return call(
        sum_kernel, "holders", [vmem, vmem], jax.ShapeDtypeStruct((SLOT_DEV, area), F32), [], 2
    )(spread, parts)


def solution(mesh):
    placed = (
        P(("grp", "row"), None, None),
        P(("grp", "row"), None),
        P(("grp", "row"), None),
        P(("grp", "row")),
        P(("grp", "row"), None),
    )
    return jax.shard_map(
        body, mesh=mesh, in_specs=placed, out_specs=P(("grp", "row"), None), check_vma=False
    )
```

```python
import functools

import jax
import jax.numpy as jnp
from jax import lax
from jax.experimental import pallas as pl
from jax.experimental.pallas import tpu as pltpu
from jax.sharding import PartitionSpec as P

BS = 64
LANES = 128
PAIRS = 32
CAP = 4
SLOT_DEV = 8
CAP2 = 4
COUNTS = 6
STEPS = (64, 32)
ASK = SUMS = tuple(reversed(range(32)))
ROWS = tuple(range(32))
QUARTERS = 4
VMEM_LIMIT = 12 * 1024 * 1024
WIDE_LIMIT = 40 * 1024 * 1024
PLAN_LIMIT = 60 * 1024 * 1024
SPARE = 1664
BF16 = jnp.bfloat16
F32 = jnp.float32


def lane_of(shape):
    return lax.broadcasted_iota(jnp.int32, shape, len(shape) - 1)


def row_of(shape):
    return lax.broadcasted_iota(jnp.int32, shape, len(shape) - 2)


def ones(mask):
    return jnp.where(mask, 1.0, 0.0).astype(BF16)


def dot(a, b, contract):
    return lax.dot_general(a, b, ((contract[:1], contract[1:]), ((), ())), preferred_element_type=F32)


def table_of(owner, local, keep, members, width):
    per_row, rows = owner.shape
    counts = jnp.zeros((members, width), F32)
    for k in range(per_row):
        of_owner = ones((row_of((members, rows)) == owner[k : k + 1]) & keep[k : k + 1])
        of_local = ones(row_of((width, rows)) == local[k : k + 1])
        counts += dot(of_owner, of_local, (1, 1))
    present = counts > 0.5
    before = ones(row_of((width, width)) < lane_of((width, width)))
    return present, dot(ones(present), before, (1, 0))


def rank_of(owner, local, rank):
    per_row, rows = owner.shape
    members, width = rank.shape
    result = jnp.zeros((per_row, rows), jnp.int32)
    for k in range(per_row):
        of_owner = ones(row_of((members, rows)) == owner[k : k + 1])
        ranks = dot(rank.astype(BF16), of_owner, (0, 0))
        mine = jnp.sum(jnp.where(row_of((width, rows)) == local[k : k + 1], ranks, 0.0), axis=0, keepdims=True)
        result = jnp.where(row_of((per_row, rows)) == k, mine.astype(jnp.int32), result)
    return result


def chosen(present, rank, cap, first, result):
    members, width = present.shape
    ids, lanes = lane_of((members, width)), lane_of((members, LANES))
    for s in range(cap):
        one = jnp.sum(jnp.where(present & (rank == float(s)), ids, 0), axis=1, keepdims=True)
        result = jnp.where(lanes == first + s, one, result)
    return result


def place_in(order, member):
    result = jnp.zeros_like(member)
    for at, who in enumerate(order):
        result = jnp.where(member == who, at, result)
    return result


def exchange(x, order):
    return lax.all_to_all(x, "row", 0, 0, tiled=True, axis_index_groups=[list(order)])


def split_cols(cols, rows, members):
    device_of = cols // rows
    return cols % rows, device_of // members, device_of % members


def plan_kernel(members, cols_ref, count_ref, slot_ref, want_ref):
    per_row, rows = cols_ref.shape
    local, group, member = split_cols(cols_ref[...], rows, members)
    live = row_of((per_row, rows)) < count_ref[...]
    slots = slot_ref[...]
    wanted = live & (group == lax.axis_index("grp")) & (member != lax.axis_index("row"))
    present, rank = table_of(place_in(ASK, member), local, wanted, members, rows)
    want = chosen(present, rank, CAP, 0, jnp.zeros((members, LANES), jnp.int32))
    holder = place_in(ASK, slots // SLOT_DEV % members)
    present, rank = table_of(holder, slots % SLOT_DEV, live, members, SLOT_DEV)
    want_ref[...] = chosen(present, rank, CAP2, CAP, want)


def lists_kernel(members, groups, cols_ref, count_ref, slot_ref, asked_ref, lists_ref, spread_ref):
    places = members * CAP2 * QUARTERS
    sender = lane_of((members, places)) // (CAP2 * QUARTERS)
    from_member = jnp.zeros((members, places), jnp.bool_)
    for at, who in enumerate(SUMS):
        from_member = from_member | ((sender == at) & (row_of((members, places)) == ASK.index(who)))
    from_member = ones(from_member)
    names = asked_ref[...][:, :SLOT_DEV].astype(F32).astype(BF16)
    named = dot(names, from_member, (0, 0))
    at = lane_of((SLOT_DEV, places))
    mine = row_of((SLOT_DEV, places)) == CAP + at // QUARTERS % CAP2
    slot_at = jnp.sum(jnp.where(mine, named, 0.0), axis=0, keepdims=True).astype(jnp.int32)
    at, to = lane_of((QUARTERS * SLOT_DEV, places)), row_of((QUARTERS * SLOT_DEV, places))
    spread_ref[...] = ones((to % SLOT_DEV == slot_at) & (to // SLOT_DEV == at % QUARTERS))

    per_row, rows = cols_ref.shape
    entries = per_row * rows
    at_k = row_of((per_row, rows))
    local, group, member = split_cols(cols_ref[...], rows, members)
    live = at_k < count_ref[...]
    slots = slot_ref[...]
    group_at = lax.axis_index("grp")
    in_group = group == group_at
    far = in_group & (member != lax.axis_index("row"))
    _, rank = table_of(member, local, live & far, members, rows)
    far_source = place_in(ROWS, member) * CAP + jnp.clip(rank_of(member, local, rank), 0, CAP - 1)
    low = group == lax.rem(group_at + groups - 1, groups)
    near_source = jnp.where(in_group, local, jnp.where(low, rows + local, 2 * rows + local))
    source = jnp.where(far, far_source, near_source)

    owner, slot = slots // SLOT_DEV % members, slots % SLOT_DEV
    _, rank = table_of(owner, slot, live, members, SLOT_DEV)
    target = place_in(SUMS, owner) * CAP2 + jnp.clip(rank_of(owner, slot, rank), 0, CAP2 - 1)

    entry = lane_of((per_row, rows)) * per_row + at_k
    before = ones(row_of((rows, rows)) < lane_of((rows, rows)))
    above = ones(lane_of((per_row, per_row)) < row_of((per_row, per_row)))
    halves = entries // LANES
    result = jnp.zeros((SLOT_DEV, LANES), jnp.int32)
    for which, mask in enumerate((live & ~far, live & far)):
        inside = dot(ones(mask), before, (1, 0))
        totals = jnp.sum(jnp.where(mask, 1.0, 0.0), axis=1, keepdims=True)
        earlier = dot(above, jnp.broadcast_to(totals, (per_row, LANES)).astype(BF16), (1, 0))[:, :1]
        at = jnp.where(mask, (inside + earlier).astype(jnp.int32), -1)
        count = jnp.sum(totals, axis=0, keepdims=True).astype(jnp.int32)
        placed = jnp.zeros((SLOT_DEV, entries), F32)
        for k in range(per_row):
            here = ones(row_of((entries, rows)) == at[k : k + 1])
            kind = row_of((SLOT_DEV, rows))
            value = jnp.where(kind == 0, entry[k : k + 1], jnp.where(kind == 1, source[k : k + 1], target[k : k + 1]))
            placed += dot(value.astype(F32).astype(BF16), here, (1, 1))
        placed = placed.astype(jnp.int32)
        code = placed[:1] * 65536 + placed[1:2] * 256 + placed[2:3]
        lanes = lane_of((1, entries))
        code = jnp.where(lanes < count, code, members * CAP2)
        kind = row_of((SLOT_DEV, LANES))
        for half in range(halves):
            part = code[:, half * LANES : (half + 1) * LANES]
            result = jnp.where(kind == which * halves + half, part, result)
        result = jnp.where(kind == COUNTS + which, count, result)
    lists_ref[...] = result


def prepare_kernel(p_ref, pq_ref, stage):
    rows = p_ref.shape[0]
    left = lane_of((rows, LANES)) < BS
    for h in range(PAIRS // 2):
        a = p_ref[:, h * LANES : (h + 1) * LANES].astype(F32)
        b = p_ref[:, (h + PAIRS // 2) * LANES : (h + PAIRS // 2 + 1) * LANES].astype(F32)
        stage[pl.ds(2 * h * rows, rows), :] = jnp.where(left, a, pltpu.roll(b, BS, 1))
        stage[pl.ds((2 * h + 1) * rows, rows), :] = jnp.where(left, pltpu.roll(a, BS, 1), b)
    for j in range(rows):
        pq_ref[j] = stage[pl.ds(j, PAIRS, stride=rows), :].astype(BF16)


def relay(a_ref, p_ref, pairs_ref, own_ref, stage, own_stage):
    rows, per_row, _ = a_ref.shape
    row_at, lane_at = row_of((LANES, LANES)), lane_of((LANES, LANES))
    col_at = row_at % BS
    order = (col_at % 2) * BS + (row_at // BS) * (BS // 2) + col_at // 2
    shuffle = ones(lane_at == order)
    for r in range(PAIRS):
        own_stage[pl.ds(r * rows, rows), :] = jnp.dot(
            p_ref[:, r * LANES : (r + 1) * LANES], shuffle, preferred_element_type=F32
        )
    at_once = LANES // PAIRS
    for first in range(0, rows, at_once):
        turned = jnp.concatenate(
            [own_stage[pl.ds(first + j, PAIRS, stride=rows), :] for j in range(at_once)], axis=0
        ).T
        for j in range(at_once):
            mine = turned[:, j * PAIRS : (j + 1) * PAIRS]
            own_ref[first + j] = jnp.concatenate(
                [mine[n * PAIRS : (n + 1) * PAIRS] for n in range(at_once)], axis=1
            ).astype(BF16)

    def one(i, carry):
        at = lax.rem(i, 2)
        for r in range(PAIRS):
            stage[at, pl.ds(r * per_row, per_row), :] = a_ref[i, :, r * LANES : (r + 1) * LANES].astype(F32)
        for k in range(per_row):
            pairs_ref[i * per_row + k] = stage[at, pl.ds(k, PAIRS, stride=per_row), :].astype(BF16)
        return carry

    lax.fori_loop(0, rows, one, 0, unroll=2)


def twice(block):
    left, zero = lane_of(block.shape) < BS, jnp.zeros(block.shape, block.dtype)
    swap = jnp.concatenate([block[:, BS:], block[:, :BS]], axis=1)
    parts = [
        jnp.where(left, block, zero),
        jnp.where(left, swap, zero),
        jnp.where(left, zero, swap),
        jnp.where(left, zero, block),
    ]
    return jnp.concatenate(parts, axis=0)


def two_products(lefts, rights):
    both = jnp.dot(
        jnp.concatenate(lefts, axis=0), jnp.concatenate(rights, axis=1), preferred_element_type=F32
    )
    return [both[:PAIRS, :LANES], both[PAIRS:, LANES:]]


def add_tiles(lists_ref, which, per_row, table_ref, pairs_ref, own_ref, total_ref):
    count = lists_ref[COUNTS + which, 0]
    first = which * (pairs_ref.shape[0] // LANES)

    def step(start, group):
        row, lane = first + start // LANES, lax.rem(start, LANES)
        codes = [lists_ref[row, lane + n] for n in range(group)]
        halves, tiles = [], []
        for n in range(0, group, 2):
            rights = [twice(table_ref[(code >> 8) & 255]) for code in codes[n : n + 2]]
            halves += two_products([pairs_ref[code >> 16] for code in codes[n : n + 2]], rights)
        for n in range(0, group, 2):
            rights = [twice(half.astype(BF16)) for half in halves[n : n + 2]]
            tiles += two_products([own_ref[(code >> 16) // per_row] for code in codes[n : n + 2]], rights)
        for code, tile in zip(codes, tiles):
            total_ref[code & 255] += tile

    large, small = STEPS
    whole = (count + large - 1 - small) // large
    rest = jnp.maximum(count - whole * large, 0)

    def one_large(n, carry):
        step(n * large, large)
        return carry

    def one_small(n, carry):
        step(whole * large + n * small, small)
        return carry

    lax.fori_loop(0, whole, one_large, 0)
    lax.fori_loop(0, (rest + small - 1) // small, one_small, 0)


def views(work_ref, per_row):
    entries = work_ref.shape[0] // (per_row + 1) * per_row
    return work_ref.at[pl.ds(0, entries)], work_ref.at[pl.ds(entries, entries // per_row)]


def clear(total_ref):
    def one(at, carry):
        total_ref[at] = jnp.zeros((PAIRS, LANES), F32)
        return carry

    lax.fori_loop(0, total_ref.shape[0], one, 0, unroll=8)


def near_kernel(per_row, lists_ref, a_ref, p_ref, pq_ref, low_ref, high_ref, work_ref, near_ref,
                table, stage, own_stage, total_ref, sem):
    pairs_ref, own_ref = views(work_ref, per_row)
    relay(a_ref, p_ref, pairs_ref, own_ref, stage, own_stage)
    rows = pq_ref.shape[0]
    for at, ref in enumerate((pq_ref, low_ref, high_ref)):
        table[pl.ds(at * rows, rows)] = ref[...]
    clear(total_ref)
    add_tiles(lists_ref, 0, per_row, table, pairs_ref, own_ref, total_ref)
    sums = total_ref.shape[0] - 1
    copy = pltpu.make_async_copy(total_ref.at[pl.ds(0, sums)], near_ref.at[pl.ds(0, sums)], sem)
    copy.start()
    copy.wait()


def far_kernel(per_row, lists_from, work_ref, got_ref, near_ref, out_ref, total, lists_ref, sem):
    blocks = total.shape[0] - 1
    copies = [
        pltpu.make_async_copy(near_ref.at[pl.ds(0, blocks)], total.at[pl.ds(0, blocks)], sem.at[0]),
        pltpu.make_async_copy(lists_from, lists_ref, sem.at[1]),
    ]
    for copy in copies:
        copy.start()
    total[blocks] = jnp.zeros((PAIRS, LANES), F32)
    pairs_ref, own_ref = views(work_ref, per_row)
    for copy in copies:
        copy.wait()
    add_tiles(lists_ref, 1, per_row, got_ref, pairs_ref, own_ref, total)
    for member in range(out_ref.shape[0]):
        for at in range(PAIRS // QUARTERS):
            rows = total.at[pl.ds(member * CAP2, CAP2)].reshape(CAP2 * PAIRS, LANES)[
                pl.ds(at, CAP2 * QUARTERS, stride=PAIRS // QUARTERS), :
            ]
            out_ref[member, :, at * LANES : (at + 1) * LANES] = rows.astype(BF16)


def pack_kernel(members, asked_ref, pq_ref, out_ref):
    for at in range(members):
        for s in range(CAP):
            out_ref[at * CAP + s] = pq_ref[asked_ref[ASK.index(ROWS[at]), s]]


def sum_kernel(spread_ref, got_ref, out_ref):
    result = jnp.dot(spread_ref[...], got_ref[...], preferred_element_type=F32)
    width = got_ref.shape[1]
    for n in range(QUARTERS):
        out_ref[:, n * width : (n + 1) * width] = result[n * SLOT_DEV : (n + 1) * SLOT_DEV]


def body(a_blocks, p_blocks, a_cols, a_count, tile_slot):
    rows, per_row, area = a_blocks.shape
    members = lax.axis_size("row")
    groups = lax.axis_size("grp")
    entries = rows * per_row
    smem = pl.BlockSpec(memory_space=pltpu.SMEM)
    vmem = pl.BlockSpec(memory_space=pltpu.VMEM)
    hbm = pl.BlockSpec(memory_space=pltpu.HBM)
    blocks = lambda n, dtype=BF16: jax.ShapeDtypeStruct((n, PAIRS, LANES), dtype)
    ints = lambda *shape: jax.ShapeDtypeStruct(shape, jnp.int32)

    def call(kernel, name, ins, outs, scratch, us, out_specs=vmem, limit=VMEM_LIMIT):
        return pl.pallas_call(
            kernel,
            out_shape=outs,
            in_specs=ins,
            out_specs=out_specs,
            scratch_shapes=scratch,
            compiler_params=pltpu.CompilerParams(vmem_limit_bytes=limit),
            cost_estimate=pl.CostEstimate(flops=0, bytes_accessed=int(us * 3e6), transcendentals=0),
            name=name,
        )

    entry = (a_cols.T, a_count.reshape(1, rows), tile_slot.T)
    want = call(
        functools.partial(plan_kernel, members), "plan", [vmem] * 3, ints(members, LANES), [], 2, limit=PLAN_LIMIT
    )(*entry)
    asked = exchange(want.reshape(members, 1, LANES), ASK).reshape(members, LANES)

    pq = call(
        prepare_kernel, "prepare", [vmem], blocks(rows), [pltpu.VMEM((PAIRS * rows, LANES), F32)], 0.1
    )(p_blocks)
    forward = [(i, (i + 1) % groups) for i in range(groups)]
    low = lax.ppermute(pq, "grp", forward)
    high = lax.ppermute(pq, "grp", [(target, source) for source, target in forward])

    send = call(
        functools.partial(pack_kernel, members), "pack", [smem, vmem], blocks(members * CAP), [], 2
    )(asked, pq)
    got = exchange(send.reshape(members, CAP, PAIRS, LANES), ROWS).reshape(members * CAP, PAIRS, LANES)

    lists, spread = call(
        functools.partial(lists_kernel, members, groups),
        "lists",
        [vmem] * 4,
        (ints(SLOT_DEV, LANES), jax.ShapeDtypeStruct((QUARTERS * SLOT_DEV, members * CAP2 * QUARTERS), BF16)),
        [],
        0.1,
        (vmem, vmem),
    )(*entry, asked)
    work, near = call(
        functools.partial(near_kernel, per_row),
        "near",
        [smem, vmem, vmem, vmem, vmem, vmem],
        (blocks(entries + rows), blocks(SPARE, F32)),
        [
            pltpu.VMEM((3 * rows, PAIRS, LANES), BF16),
            pltpu.VMEM((2, PAIRS * per_row, LANES), F32),
            pltpu.VMEM((PAIRS * rows, LANES), F32),
            pltpu.VMEM((members * CAP2 + 1, PAIRS, LANES), F32),
            pltpu.SemaphoreType.DMA,
        ],
        0.1,
        (vmem, hbm),
        WIDE_LIMIT,
    )(lists, a_blocks, p_blocks, pq, low, high)
    sums = call(
        functools.partial(far_kernel, per_row),
        "far",
        [vmem, vmem, vmem, hbm],
        jax.ShapeDtypeStruct((members, CAP2 * QUARTERS, area // QUARTERS), BF16),
        [
            pltpu.VMEM((members * CAP2 + 1, PAIRS, LANES), F32),
            pltpu.SMEM((SLOT_DEV, LANES), jnp.int32),
            pltpu.SemaphoreType.DMA((2,)),
        ],
        6,
        limit=WIDE_LIMIT,
    )(lists, work, got, near)
    parts = exchange(sums, SUMS).reshape(-1, area // QUARTERS)

    return call(
        sum_kernel, "holders", [vmem, vmem], jax.ShapeDtypeStruct((SLOT_DEV, area), F32), [], 2
    )(spread, parts)


def solution(mesh):
    placed = (
        P(("grp", "row"), None, None),
        P(("grp", "row"), None),
        P(("grp", "row"), None),
        P(("grp", "row")),
        P(("grp", "row"), None),
    )
    return jax.shard_map(
        body, mesh=mesh, in_specs=placed, out_specs=P(("grp", "row"), None), check_vma=False
    )
```

```python
import functools

import jax
import jax.numpy as jnp
from jax import lax
from jax.experimental import pallas as pl
from jax.experimental.pallas import tpu as pltpu
from jax.sharding import PartitionSpec as P

BS = 64
LANES = 128
PAIRS = 32
CAP = 4
SLOT_DEV = 8
CAP2 = 4
COUNTS = 6
STEPS = (64, 32)
ASK = SUMS = tuple(reversed(range(32)))
ROWS = tuple(range(32))
PARTS = 4
QUARTERS = 4
VMEM_LIMIT = 12 * 1024 * 1024
WIDE_LIMIT = 40 * 1024 * 1024
PLAN_LIMIT = 60 * 1024 * 1024
SPARE = 1664
BF16 = jnp.bfloat16
F32 = jnp.float32


def lane_of(shape):
    return lax.broadcasted_iota(jnp.int32, shape, len(shape) - 1)


def row_of(shape):
    return lax.broadcasted_iota(jnp.int32, shape, len(shape) - 2)


def ones(mask):
    return jnp.where(mask, 1.0, 0.0).astype(BF16)


def dot(a, b, contract):
    return lax.dot_general(a, b, ((contract[:1], contract[1:]), ((), ())), preferred_element_type=F32)


def table_of(owner, local, keep, members, width):
    per_row, rows = owner.shape
    counts = jnp.zeros((members, width), F32)
    for k in range(per_row):
        of_owner = ones((row_of((members, rows)) == owner[k : k + 1]) & keep[k : k + 1])
        of_local = ones(row_of((width, rows)) == local[k : k + 1])
        counts += dot(of_owner, of_local, (1, 1))
    present = counts > 0.5
    before = ones(row_of((width, width)) < lane_of((width, width)))
    return present, dot(ones(present), before, (1, 0))


def rank_of(owner, local, rank):
    per_row, rows = owner.shape
    members, width = rank.shape
    result = jnp.zeros((per_row, rows), jnp.int32)
    for k in range(per_row):
        of_owner = ones(row_of((members, rows)) == owner[k : k + 1])
        ranks = dot(rank.astype(BF16), of_owner, (0, 0))
        mine = jnp.sum(jnp.where(row_of((width, rows)) == local[k : k + 1], ranks, 0.0), axis=0, keepdims=True)
        result = jnp.where(row_of((per_row, rows)) == k, mine.astype(jnp.int32), result)
    return result


def chosen(present, rank, cap, first, result):
    members, width = present.shape
    ids, lanes = lane_of((members, width)), lane_of((members, LANES))
    for s in range(cap):
        one = jnp.sum(jnp.where(present & (rank == float(s)), ids, 0), axis=1, keepdims=True)
        result = jnp.where(lanes == first + s, one, result)
    return result


def place_in(order, member):
    result = jnp.zeros_like(member)
    for at, who in enumerate(order):
        result = jnp.where(member == who, at, result)
    return result


def exchange(x, order):
    return lax.all_to_all(x, "row", 0, 0, tiled=True, axis_index_groups=[list(order)])


def split_cols(cols, rows, members):
    device_of = cols // rows
    return cols % rows, device_of // members, device_of % members


def plan_kernel(members, cols_ref, count_ref, slot_ref, want_ref):
    per_row, rows = cols_ref.shape
    local, group, member = split_cols(cols_ref[...], rows, members)
    live = row_of((per_row, rows)) < count_ref[...]
    slots = slot_ref[...]
    wanted = live & (group == lax.axis_index("grp")) & (member != lax.axis_index("row"))
    present, rank = table_of(place_in(ASK, member), local, wanted, members, rows)
    want = chosen(present, rank, CAP, 0, jnp.zeros((members, LANES), jnp.int32))
    holder = place_in(ASK, slots // SLOT_DEV % members)
    present, rank = table_of(holder, slots % SLOT_DEV, live, members, SLOT_DEV)
    want_ref[...] = chosen(present, rank, CAP2, CAP, want)


def lists_kernel(members, groups, cols_ref, count_ref, slot_ref, asked_ref, lists_ref, spread_ref):
    places = members * CAP2 * QUARTERS
    sender = lane_of((members, places)) // (CAP2 * QUARTERS)
    from_member = jnp.zeros((members, places), jnp.bool_)
    for at, who in enumerate(SUMS):
        from_member = from_member | ((sender == at) & (row_of((members, places)) == ASK.index(who)))
    from_member = ones(from_member)
    names = asked_ref[...][:, :SLOT_DEV].astype(F32).astype(BF16)
    named = dot(names, from_member, (0, 0))
    at = lane_of((SLOT_DEV, places))
    mine = row_of((SLOT_DEV, places)) == CAP + at // QUARTERS % CAP2
    slot_at = jnp.sum(jnp.where(mine, named, 0.0), axis=0, keepdims=True).astype(jnp.int32)
    at, to = lane_of((QUARTERS * SLOT_DEV, places)), row_of((QUARTERS * SLOT_DEV, places))
    spread_ref[...] = ones((to % SLOT_DEV == slot_at) & (to // SLOT_DEV == at % QUARTERS))

    per_row, rows = cols_ref.shape
    entries = per_row * rows
    at_k = row_of((per_row, rows))
    local, group, member = split_cols(cols_ref[...], rows, members)
    live = at_k < count_ref[...]
    slots = slot_ref[...]
    group_at = lax.axis_index("grp")
    in_group = group == group_at
    far = in_group & (member != lax.axis_index("row"))
    _, rank = table_of(member, local, live & far, members, rows)
    far_source = place_in(ROWS, member) * CAP + jnp.clip(rank_of(member, local, rank), 0, CAP - 1)
    low = group == lax.rem(group_at + groups - 1, groups)
    near_source = jnp.where(in_group, local, jnp.where(low, rows + local, 2 * rows + local))
    source = jnp.where(far, far_source, near_source)

    owner, slot = slots // SLOT_DEV % members, slots % SLOT_DEV
    _, rank = table_of(owner, slot, live, members, SLOT_DEV)
    target = place_in(SUMS, owner) * CAP2 + jnp.clip(rank_of(owner, slot, rank), 0, CAP2 - 1)

    entry = lane_of((per_row, rows)) * per_row + at_k
    before = ones(row_of((rows, rows)) < lane_of((rows, rows)))
    above = ones(lane_of((per_row, per_row)) < row_of((per_row, per_row)))
    halves = entries // LANES
    result = jnp.zeros((SLOT_DEV, LANES), jnp.int32)
    for which, mask in enumerate((live & ~far, live & far)):
        inside = dot(ones(mask), before, (1, 0))
        totals = jnp.sum(jnp.where(mask, 1.0, 0.0), axis=1, keepdims=True)
        earlier = dot(above, jnp.broadcast_to(totals, (per_row, LANES)).astype(BF16), (1, 0))[:, :1]
        at = jnp.where(mask, (inside + earlier).astype(jnp.int32), -1)
        count = jnp.sum(totals, axis=0, keepdims=True).astype(jnp.int32)
        placed = jnp.zeros((SLOT_DEV, entries), F32)
        for k in range(per_row):
            here = ones(row_of((entries, rows)) == at[k : k + 1])
            kind = row_of((SLOT_DEV, rows))
            value = jnp.where(kind == 0, entry[k : k + 1], jnp.where(kind == 1, source[k : k + 1], target[k : k + 1]))
            placed += dot(value.astype(F32).astype(BF16), here, (1, 1))
        placed = placed.astype(jnp.int32)
        code = placed[:1] * 65536 + placed[1:2] * 256 + placed[2:3]
        lanes = lane_of((1, entries))
        code = jnp.where(lanes < count, code, members * CAP2)
        kind = row_of((SLOT_DEV, LANES))
        for half in range(halves):
            part = code[:, half * LANES : (half + 1) * LANES]
            result = jnp.where(kind == which * halves + half, part, result)
        result = jnp.where(kind == COUNTS + which, count, result)
    lists_ref[...] = result


def prepare_kernel(p_ref, pq_ref, stage):
    rows = p_ref.shape[0]
    left = lane_of((rows, LANES)) < BS
    for h in range(PAIRS // 2):
        a = p_ref[:, h * LANES : (h + 1) * LANES].astype(F32)
        b = p_ref[:, (h + PAIRS // 2) * LANES : (h + PAIRS // 2 + 1) * LANES].astype(F32)
        stage[pl.ds(2 * h * rows, rows), :] = jnp.where(left, a, pltpu.roll(b, BS, 1))
        stage[pl.ds((2 * h + 1) * rows, rows), :] = jnp.where(left, pltpu.roll(a, BS, 1), b)
    for j in range(rows):
        pq_ref[j] = stage[pl.ds(j, PAIRS, stride=rows), :].astype(BF16)


def relay(a_ref, p_ref, pairs_ref, own_ref, stage, own_stage):
    rows, per_row, _ = a_ref.shape
    row_at, lane_at = row_of((LANES, LANES)), lane_of((LANES, LANES))
    col_at = row_at % BS
    order = (col_at % 2) * BS + (row_at // BS) * (BS // 2) + col_at // 2
    shuffle = ones(lane_at == order)
    for r in range(PAIRS):
        own_stage[pl.ds(r * rows, rows), :] = jnp.dot(
            p_ref[:, r * LANES : (r + 1) * LANES], shuffle, preferred_element_type=F32
        )
    at_once = LANES // PAIRS
    for first in range(0, rows, at_once):
        turned = jnp.concatenate(
            [own_stage[pl.ds(first + j, PAIRS, stride=rows), :] for j in range(at_once)], axis=0
        ).T
        for j in range(at_once):
            mine = turned[:, j * PAIRS : (j + 1) * PAIRS]
            own_ref[first + j] = jnp.concatenate(
                [mine[n * PAIRS : (n + 1) * PAIRS] for n in range(at_once)], axis=1
            ).astype(BF16)

    def one(i, carry):
        at = lax.rem(i, 2)
        for r in range(PAIRS):
            stage[at, pl.ds(r * per_row, per_row), :] = a_ref[i, :, r * LANES : (r + 1) * LANES].astype(F32)
        for k in range(per_row):
            pairs_ref[i * per_row + k] = stage[at, pl.ds(k, PAIRS, stride=per_row), :].astype(BF16)
        return carry

    lax.fori_loop(0, rows, one, 0, unroll=2)


def twice(block):
    left, zero = lane_of(block.shape) < BS, jnp.zeros(block.shape, block.dtype)
    swap = jnp.concatenate([block[:, BS:], block[:, :BS]], axis=1)
    parts = [
        jnp.where(left, block, zero),
        jnp.where(left, swap, zero),
        jnp.where(left, zero, swap),
        jnp.where(left, zero, block),
    ]
    return jnp.concatenate(parts, axis=0)


def two_products(lefts, rights):
    both = jnp.dot(
        jnp.concatenate(lefts, axis=0), jnp.concatenate(rights, axis=1), preferred_element_type=F32
    )
    return [both[:PAIRS, :LANES], both[PAIRS:, LANES:]]


def add_tiles(lists_ref, which, per_row, table_ref, pairs_ref, own_ref, total_ref):
    count = lists_ref[COUNTS + which, 0]
    first = which * (pairs_ref.shape[0] // LANES)

    def step(start, group):
        row, lane = first + start // LANES, lax.rem(start, LANES)
        codes = [lists_ref[row, lane + n] for n in range(group)]
        halves, tiles = [], []
        for n in range(0, group, 2):
            rights = [twice(table_ref[(code >> 8) & 255]) for code in codes[n : n + 2]]
            halves += two_products([pairs_ref[code >> 16] for code in codes[n : n + 2]], rights)
        for n in range(0, group, 2):
            rights = [twice(half.astype(BF16)) for half in halves[n : n + 2]]
            tiles += two_products([own_ref[(code >> 16) // per_row] for code in codes[n : n + 2]], rights)
        for code, tile in zip(codes, tiles):
            total_ref[code & 255] += tile

    large, small = STEPS
    whole = (count + large - 1 - small) // large
    rest = jnp.maximum(count - whole * large, 0)

    def one_large(n, carry):
        step(n * large, large)
        return carry

    def one_small(n, carry):
        step(whole * large + n * small, small)
        return carry

    lax.fori_loop(0, whole, one_large, 0)
    lax.fori_loop(0, (rest + small - 1) // small, one_small, 0)


def views(work_ref, per_row):
    entries = work_ref.shape[0] // (per_row + 1) * per_row
    return work_ref.at[pl.ds(0, entries)], work_ref.at[pl.ds(entries, entries // per_row)]


def clear(total_ref):
    def one(at, carry):
        total_ref[at] = jnp.zeros((PAIRS, LANES), F32)
        return carry

    lax.fori_loop(0, total_ref.shape[0], one, 0, unroll=8)


def near_kernel(per_row, lists_ref, a_ref, p_ref, pq_ref, low_ref, high_ref, work_ref, near_ref,
                table, stage, own_stage, total_ref, sem):
    pairs_ref, own_ref = views(work_ref, per_row)
    relay(a_ref, p_ref, pairs_ref, own_ref, stage, own_stage)
    rows = pq_ref.shape[0]
    for at, ref in enumerate((pq_ref, low_ref, high_ref)):
        table[pl.ds(at * rows, rows)] = ref[...]
    clear(total_ref)
    add_tiles(lists_ref, 0, per_row, table, pairs_ref, own_ref, total_ref)
    sums = total_ref.shape[0] - 1
    copy = pltpu.make_async_copy(total_ref.at[pl.ds(0, sums)], near_ref.at[pl.ds(0, sums)], sem)
    copy.start()
    copy.wait()


def far_kernel(per_row, lists_from, work_ref, got_ref, near_ref, out_ref, total, lists_ref, sem):
    blocks = total.shape[0] - 1
    copies = [
        pltpu.make_async_copy(near_ref.at[pl.ds(0, blocks)], total.at[pl.ds(0, blocks)], sem.at[0]),
        pltpu.make_async_copy(lists_from, lists_ref, sem.at[1]),
    ]
    for copy in copies:
        copy.start()
    total[blocks] = jnp.zeros((PAIRS, LANES), F32)
    pairs_ref, own_ref = views(work_ref, per_row)
    for copy in copies:
        copy.wait()
    add_tiles(lists_ref, 1, per_row, got_ref, pairs_ref, own_ref, total)
    for member in range(out_ref.shape[0]):
        for at in range(PAIRS // QUARTERS):
            rows = total.at[pl.ds(member * CAP2, CAP2)].reshape(CAP2 * PAIRS, LANES)[
                pl.ds(at, CAP2 * QUARTERS, stride=PAIRS // QUARTERS), :
            ]
            out_ref[member, :, at * LANES : (at + 1) * LANES] = rows.astype(BF16)


def pack_kernel(members, asked_from, pq_ref, out_ref, asked_ref, sem):
    share = members // PARTS
    copies = [
        pltpu.make_async_copy(
            asked_from.at[pl.ds(n * share, share)], asked_ref.at[pl.ds(n * share, share)], sem.at[n]
        )
        for n in range(PARTS)
    ]
    for copy in copies:
        copy.start()
    for n, copy in enumerate(copies):
        copy.wait()
        for row in range(n * share, (n + 1) * share):
            at = ROWS.index(ASK[row])
            for s in range(CAP):
                out_ref[at * CAP + s] = pq_ref[asked_ref[row, s]]


def sum_kernel(spread_ref, got_ref, out_ref):
    result = jnp.dot(spread_ref[...], got_ref[...], preferred_element_type=F32)
    width = got_ref.shape[1]
    for n in range(QUARTERS):
        out_ref[:, n * width : (n + 1) * width] = result[n * SLOT_DEV : (n + 1) * SLOT_DEV]


def body(a_blocks, p_blocks, a_cols, a_count, tile_slot):
    rows, per_row, area = a_blocks.shape
    members = lax.axis_size("row")
    groups = lax.axis_size("grp")
    entries = rows * per_row
    smem = pl.BlockSpec(memory_space=pltpu.SMEM)
    vmem = pl.BlockSpec(memory_space=pltpu.VMEM)
    hbm = pl.BlockSpec(memory_space=pltpu.HBM)
    blocks = lambda n, dtype=BF16: jax.ShapeDtypeStruct((n, PAIRS, LANES), dtype)
    ints = lambda *shape: jax.ShapeDtypeStruct(shape, jnp.int32)

    def call(kernel, name, ins, outs, scratch, us, out_specs=vmem, limit=VMEM_LIMIT):
        return pl.pallas_call(
            kernel,
            out_shape=outs,
            in_specs=ins,
            out_specs=out_specs,
            scratch_shapes=scratch,
            compiler_params=pltpu.CompilerParams(vmem_limit_bytes=limit),
            cost_estimate=pl.CostEstimate(flops=0, bytes_accessed=int(us * 3e6), transcendentals=0),
            name=name,
        )

    entry = (a_cols.T, a_count.reshape(1, rows), tile_slot.T)
    want = call(
        functools.partial(plan_kernel, members), "plan", [vmem] * 3, ints(members, LANES), [], 2, limit=PLAN_LIMIT
    )(*entry)
    asked = exchange(want.reshape(members, 1, LANES), ASK).reshape(members, LANES)

    pq = call(
        prepare_kernel, "prepare", [vmem], blocks(rows), [pltpu.VMEM(((PAIRS + 1) * rows, LANES), F32)], 0.1
    )(p_blocks)
    forward = [(i, (i + 1) % groups) for i in range(groups)]
    low = lax.ppermute(pq, "grp", forward)
    high = lax.ppermute(pq, "grp", [(target, source) for source, target in forward])

    send = call(
        functools.partial(pack_kernel, members), "pack", [vmem, vmem], blocks(members * CAP),
        [pltpu.SMEM((members, LANES), jnp.int32), pltpu.SemaphoreType.DMA((PARTS,))], 2
    )(asked, pq)
    got = exchange(send.reshape(members, CAP, PAIRS, LANES), ROWS).reshape(members * CAP, PAIRS, LANES)

    lists, spread = call(
        functools.partial(lists_kernel, members, groups),
        "lists",
        [vmem] * 4,
        (ints(SLOT_DEV, LANES), jax.ShapeDtypeStruct((QUARTERS * SLOT_DEV, members * CAP2 * QUARTERS), BF16)),
        [],
        0.1,
        (vmem, vmem),
    )(*entry, asked)
    work, near = call(
        functools.partial(near_kernel, per_row),
        "near",
        [smem, vmem, vmem, vmem, vmem, vmem],
        (blocks(entries + rows), blocks(SPARE, F32)),
        [
            pltpu.VMEM((3 * rows, PAIRS, LANES), BF16),
            pltpu.VMEM((2, (PAIRS + 1) * per_row, LANES), F32),
            pltpu.VMEM(((PAIRS + 1) * rows, LANES), F32),
            pltpu.VMEM((members * CAP2 + 1, PAIRS, LANES), F32),
            pltpu.SemaphoreType.DMA,
        ],
        0.1,
        (vmem, hbm),
        WIDE_LIMIT,
    )(lists, a_blocks, p_blocks, pq, low, high)
    sums = call(
        functools.partial(far_kernel, per_row),
        "far",
        [vmem, vmem, vmem, hbm],
        jax.ShapeDtypeStruct((members, CAP2 * QUARTERS, area // QUARTERS), BF16),
        [
            pltpu.VMEM((members * CAP2 + 1, PAIRS, LANES), F32),
            pltpu.SMEM((SLOT_DEV, LANES), jnp.int32),
            pltpu.SemaphoreType.DMA((2,)),
        ],
        6,
        limit=WIDE_LIMIT,
    )(lists, work, got, near)
    parts = exchange(sums, SUMS).reshape(-1, area // QUARTERS)

    return call(
        sum_kernel, "holders", [vmem, vmem], jax.ShapeDtypeStruct((SLOT_DEV, area), F32), [], 2
    )(spread, parts)


def solution(mesh):
    placed = (
        P(("grp", "row"), None, None),
        P(("grp", "row"), None),
        P(("grp", "row"), None),
        P(("grp", "row")),
        P(("grp", "row"), None),
    )
    return jax.shard_map(
        body, mesh=mesh, in_specs=placed, out_specs=P(("grp", "row"), None), check_vma=False
    )
```

```python
import functools

import jax
import jax.numpy as jnp
from jax import lax
from jax.experimental import pallas as pl
from jax.experimental.pallas import tpu as pltpu
from jax.sharding import PartitionSpec as P

BS = 64
LANES = 128
PAIRS = 32
CAP = 4
SLOT_DEV = 8
CAP2 = 4
COUNTS = 6
STEPS = (64, 32)
ASK = tuple(reversed(range(32)))
SUMS = tuple(z * 4 + y for z in reversed(range(8)) for y in range(4))
ROWS = tuple(range(32))
PARTS = 4
QUARTERS = 4
VMEM_LIMIT = 12 * 1024 * 1024
WIDE_LIMIT = 40 * 1024 * 1024
PLAN_LIMIT = 60 * 1024 * 1024
SPARE = 1664
BF16 = jnp.bfloat16
F32 = jnp.float32


def lane_of(shape):
    return lax.broadcasted_iota(jnp.int32, shape, len(shape) - 1)


def row_of(shape):
    return lax.broadcasted_iota(jnp.int32, shape, len(shape) - 2)


def ones(mask):
    return jnp.where(mask, 1.0, 0.0).astype(BF16)


def dot(a, b, contract):
    return lax.dot_general(a, b, ((contract[:1], contract[1:]), ((), ())), preferred_element_type=F32)


def table_of(owner, local, keep, members, width):
    per_row, rows = owner.shape
    counts = jnp.zeros((members, width), F32)
    for k in range(per_row):
        of_owner = ones((row_of((members, rows)) == owner[k : k + 1]) & keep[k : k + 1])
        of_local = ones(row_of((width, rows)) == local[k : k + 1])
        counts += dot(of_owner, of_local, (1, 1))
    present = counts > 0.5
    before = ones(row_of((width, width)) < lane_of((width, width)))
    return present, dot(ones(present), before, (1, 0))


def rank_of(owner, local, rank):
    per_row, rows = owner.shape
    members, width = rank.shape
    result = jnp.zeros((per_row, rows), jnp.int32)
    for k in range(per_row):
        of_owner = ones(row_of((members, rows)) == owner[k : k + 1])
        ranks = dot(rank.astype(BF16), of_owner, (0, 0))
        mine = jnp.sum(jnp.where(row_of((width, rows)) == local[k : k + 1], ranks, 0.0), axis=0, keepdims=True)
        result = jnp.where(row_of((per_row, rows)) == k, mine.astype(jnp.int32), result)
    return result


def chosen(present, rank, cap, first, result):
    members, width = present.shape
    ids, lanes = lane_of((members, width)), lane_of((members, LANES))
    for s in range(cap):
        one = jnp.sum(jnp.where(present & (rank == float(s)), ids, 0), axis=1, keepdims=True)
        result = jnp.where(lanes == first + s, one, result)
    return result


def place_in(order, member):
    result = jnp.zeros_like(member)
    for at, who in enumerate(order):
        result = jnp.where(member == who, at, result)
    return result


def exchange(x, order):
    return lax.all_to_all(x, "row", 0, 0, tiled=True, axis_index_groups=[list(order)])


def split_cols(cols, rows, members):
    device_of = cols // rows
    return cols % rows, device_of // members, device_of % members


def plan_kernel(members, cols_ref, count_ref, slot_ref, want_ref):
    per_row, rows = cols_ref.shape
    local, group, member = split_cols(cols_ref[...], rows, members)
    live = row_of((per_row, rows)) < count_ref[...]
    slots = slot_ref[...]
    wanted = live & (group == lax.axis_index("grp")) & (member != lax.axis_index("row"))
    present, rank = table_of(place_in(ASK, member), local, wanted, members, rows)
    want = chosen(present, rank, CAP, 0, jnp.zeros((members, LANES), jnp.int32))
    holder = place_in(ASK, slots // SLOT_DEV % members)
    present, rank = table_of(holder, slots % SLOT_DEV, live, members, SLOT_DEV)
    want_ref[...] = chosen(present, rank, CAP2, CAP, want)


def lists_kernel(members, groups, cols_ref, count_ref, slot_ref, asked_ref, lists_ref, spread_ref):
    places = members * CAP2 * QUARTERS
    sender = lane_of((members, places)) // (CAP2 * QUARTERS)
    from_member = jnp.zeros((members, places), jnp.bool_)
    for at, who in enumerate(SUMS):
        from_member = from_member | ((sender == at) & (row_of((members, places)) == ASK.index(who)))
    from_member = ones(from_member)
    names = asked_ref[...][:, :SLOT_DEV].astype(F32).astype(BF16)
    named = dot(names, from_member, (0, 0))
    at = lane_of((SLOT_DEV, places))
    mine = row_of((SLOT_DEV, places)) == CAP + at // QUARTERS % CAP2
    slot_at = jnp.sum(jnp.where(mine, named, 0.0), axis=0, keepdims=True).astype(jnp.int32)
    at, to = lane_of((QUARTERS * SLOT_DEV, places)), row_of((QUARTERS * SLOT_DEV, places))
    spread_ref[...] = ones((to % SLOT_DEV == slot_at) & (to // SLOT_DEV == at % QUARTERS))

    per_row, rows = cols_ref.shape
    entries = per_row * rows
    at_k = row_of((per_row, rows))
    local, group, member = split_cols(cols_ref[...], rows, members)
    live = at_k < count_ref[...]
    slots = slot_ref[...]
    group_at = lax.axis_index("grp")
    in_group = group == group_at
    far = in_group & (member != lax.axis_index("row"))
    _, rank = table_of(member, local, live & far, members, rows)
    far_source = place_in(ROWS, member) * CAP + jnp.clip(rank_of(member, local, rank), 0, CAP - 1)
    low = group == lax.rem(group_at + groups - 1, groups)
    near_source = jnp.where(in_group, local, jnp.where(low, rows + local, 2 * rows + local))
    source = jnp.where(far, far_source, near_source)

    owner, slot = slots // SLOT_DEV % members, slots % SLOT_DEV
    _, rank = table_of(owner, slot, live, members, SLOT_DEV)
    target = place_in(SUMS, owner) * CAP2 + jnp.clip(rank_of(owner, slot, rank), 0, CAP2 - 1)

    entry = lane_of((per_row, rows)) * per_row + at_k
    before = ones(row_of((rows, rows)) < lane_of((rows, rows)))
    above = ones(lane_of((per_row, per_row)) < row_of((per_row, per_row)))
    halves = entries // LANES
    result = jnp.zeros((SLOT_DEV, LANES), jnp.int32)
    for which, mask in enumerate((live & ~far, live & far)):
        inside = dot(ones(mask), before, (1, 0))
        totals = jnp.sum(jnp.where(mask, 1.0, 0.0), axis=1, keepdims=True)
        earlier = dot(above, jnp.broadcast_to(totals, (per_row, LANES)).astype(BF16), (1, 0))[:, :1]
        at = jnp.where(mask, (inside + earlier).astype(jnp.int32), -1)
        count = jnp.sum(totals, axis=0, keepdims=True).astype(jnp.int32)
        placed = jnp.zeros((SLOT_DEV, entries), F32)
        for k in range(per_row):
            here = ones(row_of((entries, rows)) == at[k : k + 1])
            kind = row_of((SLOT_DEV, rows))
            value = jnp.where(kind == 0, entry[k : k + 1], jnp.where(kind == 1, source[k : k + 1], target[k : k + 1]))
            placed += dot(value.astype(F32).astype(BF16), here, (1, 1))
        placed = placed.astype(jnp.int32)
        code = placed[:1] * 65536 + placed[1:2] * 256 + placed[2:3]
        lanes = lane_of((1, entries))
        code = jnp.where(lanes < count, code, members * CAP2)
        kind = row_of((SLOT_DEV, LANES))
        for half in range(halves):
            part = code[:, half * LANES : (half + 1) * LANES]
            result = jnp.where(kind == which * halves + half, part, result)
        result = jnp.where(kind == COUNTS + which, count, result)
    lists_ref[...] = result


def prepare_kernel(p_ref, pq_ref, stage):
    rows = p_ref.shape[0]
    left = lane_of((rows, LANES)) < BS
    for h in range(PAIRS // 2):
        a = p_ref[:, h * LANES : (h + 1) * LANES].astype(F32)
        b = p_ref[:, (h + PAIRS // 2) * LANES : (h + PAIRS // 2 + 1) * LANES].astype(F32)
        stage[pl.ds(2 * h * rows, rows), :] = jnp.where(left, a, pltpu.roll(b, BS, 1))
        stage[pl.ds((2 * h + 1) * rows, rows), :] = jnp.where(left, pltpu.roll(a, BS, 1), b)
    for j in range(rows):
        pq_ref[j] = stage[pl.ds(j, PAIRS, stride=rows), :].astype(BF16)


def relay(a_ref, p_ref, pairs_ref, own_ref, stage, own_stage):
    rows, per_row, _ = a_ref.shape
    row_at, lane_at = row_of((LANES, LANES)), lane_of((LANES, LANES))
    col_at = row_at % BS
    order = (col_at % 2) * BS + (row_at // BS) * (BS // 2) + col_at // 2
    shuffle = ones(lane_at == order)
    for r in range(PAIRS):
        own_stage[pl.ds(r * rows, rows), :] = jnp.dot(
            p_ref[:, r * LANES : (r + 1) * LANES], shuffle, preferred_element_type=F32
        )
    at_once = LANES // PAIRS
    for first in range(0, rows, at_once):
        turned = jnp.concatenate(
            [own_stage[pl.ds(first + j, PAIRS, stride=rows), :] for j in range(at_once)], axis=0
        ).T
        for j in range(at_once):
            mine = turned[:, j * PAIRS : (j + 1) * PAIRS]
            own_ref[first + j] = jnp.concatenate(
                [mine[n * PAIRS : (n + 1) * PAIRS] for n in range(at_once)], axis=1
            ).astype(BF16)

    def one(i, carry):
        at = lax.rem(i, 2)
        for r in range(PAIRS):
            stage[at, pl.ds(r * per_row, per_row), :] = a_ref[i, :, r * LANES : (r + 1) * LANES].astype(F32)
        for k in range(per_row):
            pairs_ref[i * per_row + k] = stage[at, pl.ds(k, PAIRS, stride=per_row), :].astype(BF16)
        return carry

    lax.fori_loop(0, rows, one, 0, unroll=2)


def twice(block):
    left, zero = lane_of(block.shape) < BS, jnp.zeros(block.shape, block.dtype)
    swap = jnp.concatenate([block[:, BS:], block[:, :BS]], axis=1)
    parts = [
        jnp.where(left, block, zero),
        jnp.where(left, swap, zero),
        jnp.where(left, zero, swap),
        jnp.where(left, zero, block),
    ]
    return jnp.concatenate(parts, axis=0)


def two_products(lefts, rights):
    both = jnp.dot(
        jnp.concatenate(lefts, axis=0), jnp.concatenate(rights, axis=1), preferred_element_type=F32
    )
    return [both[:PAIRS, :LANES], both[PAIRS:, LANES:]]


def add_tiles(lists_ref, which, per_row, table_ref, pairs_ref, own_ref, total_ref):
    count = lists_ref[COUNTS + which, 0]
    first = which * (pairs_ref.shape[0] // LANES)

    def step(start, group):
        row, lane = first + start // LANES, lax.rem(start, LANES)
        codes = [lists_ref[row, lane + n] for n in range(group)]
        halves, tiles = [], []
        for n in range(0, group, 2):
            rights = [twice(table_ref[(code >> 8) & 255]) for code in codes[n : n + 2]]
            halves += two_products([pairs_ref[code >> 16] for code in codes[n : n + 2]], rights)
        for n in range(0, group, 2):
            rights = [twice(half.astype(BF16)) for half in halves[n : n + 2]]
            tiles += two_products([own_ref[(code >> 16) // per_row] for code in codes[n : n + 2]], rights)
        for code, tile in zip(codes, tiles):
            total_ref[code & 255] += tile

    large, small = STEPS
    whole = (count + large - 1 - small) // large
    rest = jnp.maximum(count - whole * large, 0)

    def one_large(n, carry):
        step(n * large, large)
        return carry

    def one_small(n, carry):
        step(whole * large + n * small, small)
        return carry

    lax.fori_loop(0, whole, one_large, 0)
    lax.fori_loop(0, (rest + small - 1) // small, one_small, 0)


def views(work_ref, per_row):
    entries = work_ref.shape[0] // (per_row + 1) * per_row
    return work_ref.at[pl.ds(0, entries)], work_ref.at[pl.ds(entries, entries // per_row)]


def clear(total_ref):
    def one(at, carry):
        total_ref[at] = jnp.zeros((PAIRS, LANES), F32)
        return carry

    lax.fori_loop(0, total_ref.shape[0], one, 0, unroll=8)


def near_kernel(per_row, lists_ref, a_ref, p_ref, pq_ref, low_ref, high_ref, work_ref, near_ref,
                table, stage, own_stage, total_ref, sem):
    pairs_ref, own_ref = views(work_ref, per_row)
    relay(a_ref, p_ref, pairs_ref, own_ref, stage, own_stage)
    rows = pq_ref.shape[0]
    for at, ref in enumerate((pq_ref, low_ref, high_ref)):
        table[pl.ds(at * rows, rows)] = ref[...]
    clear(total_ref)
    add_tiles(lists_ref, 0, per_row, table, pairs_ref, own_ref, total_ref)
    sums = total_ref.shape[0] - 1
    copy = pltpu.make_async_copy(total_ref.at[pl.ds(0, sums)], near_ref.at[pl.ds(0, sums)], sem)
    copy.start()
    copy.wait()


def far_kernel(per_row, lists_from, work_ref, got_ref, near_ref, out_ref, total, lists_ref, sem):
    blocks = total.shape[0] - 1
    copies = [
        pltpu.make_async_copy(near_ref.at[pl.ds(0, blocks)], total.at[pl.ds(0, blocks)], sem.at[0]),
        pltpu.make_async_copy(lists_from, lists_ref, sem.at[1]),
    ]
    for copy in copies:
        copy.start()
    total[blocks] = jnp.zeros((PAIRS, LANES), F32)
    pairs_ref, own_ref = views(work_ref, per_row)
    for copy in copies:
        copy.wait()
    add_tiles(lists_ref, 1, per_row, got_ref, pairs_ref, own_ref, total)
    for member in range(out_ref.shape[0]):
        for at in range(PAIRS // QUARTERS):
            rows = total.at[pl.ds(member * CAP2, CAP2)].reshape(CAP2 * PAIRS, LANES)[
                pl.ds(at, CAP2 * QUARTERS, stride=PAIRS // QUARTERS), :
            ]
            out_ref[member, :, at * LANES : (at + 1) * LANES] = rows.astype(BF16)


def pack_kernel(members, asked_from, pq_ref, out_ref, asked_ref, sem):
    share = members // PARTS
    copies = [
        pltpu.make_async_copy(
            asked_from.at[pl.ds(n * share, share)], asked_ref.at[pl.ds(n * share, share)], sem.at[n]
        )
        for n in range(PARTS)
    ]
    for copy in copies:
        copy.start()
    for n, copy in enumerate(copies):
        copy.wait()
        for row in range(n * share, (n + 1) * share):
            at = ROWS.index(ASK[row])
            for s in range(CAP):
                out_ref[at * CAP + s] = pq_ref[asked_ref[row, s]]


def sum_kernel(spread_ref, got_ref, out_ref):
    result = jnp.dot(spread_ref[...], got_ref[...], preferred_element_type=F32)
    width = got_ref.shape[1]
    for n in range(QUARTERS):
        out_ref[:, n * width : (n + 1) * width] = result[n * SLOT_DEV : (n + 1) * SLOT_DEV]


def body(a_blocks, p_blocks, a_cols, a_count, tile_slot):
    rows, per_row, area = a_blocks.shape
    members = lax.axis_size("row")
    groups = lax.axis_size("grp")
    entries = rows * per_row
    smem = pl.BlockSpec(memory_space=pltpu.SMEM)
    vmem = pl.BlockSpec(memory_space=pltpu.VMEM)
    hbm = pl.BlockSpec(memory_space=pltpu.HBM)
    blocks = lambda n, dtype=BF16: jax.ShapeDtypeStruct((n, PAIRS, LANES), dtype)
    ints = lambda *shape: jax.ShapeDtypeStruct(shape, jnp.int32)

    def call(kernel, name, ins, outs, scratch, us, out_specs=vmem, limit=VMEM_LIMIT):
        return pl.pallas_call(
            kernel,
            out_shape=outs,
            in_specs=ins,
            out_specs=out_specs,
            scratch_shapes=scratch,
            compiler_params=pltpu.CompilerParams(vmem_limit_bytes=limit),
            cost_estimate=pl.CostEstimate(flops=0, bytes_accessed=int(us * 3e6), transcendentals=0),
            name=name,
        )

    entry = (a_cols.T, a_count.reshape(1, rows), tile_slot.T)
    want = call(
        functools.partial(plan_kernel, members), "plan", [vmem] * 3, ints(members, LANES), [], 2, limit=PLAN_LIMIT
    )(*entry)
    asked = exchange(want.reshape(members, 1, LANES), ASK).reshape(members, LANES)

    pq = call(
        prepare_kernel, "prepare", [vmem], blocks(rows), [pltpu.VMEM(((PAIRS + 1) * rows, LANES), F32)], 0.1
    )(p_blocks)
    forward = [(i, (i + 1) % groups) for i in range(groups)]
    low = lax.ppermute(pq, "grp", forward)
    high = lax.ppermute(pq, "grp", [(target, source) for source, target in forward])

    send = call(
        functools.partial(pack_kernel, members), "pack", [vmem, vmem], blocks(members * CAP),
        [pltpu.SMEM((members, LANES), jnp.int32), pltpu.SemaphoreType.DMA((PARTS,))], 2
    )(asked, pq)
    got = exchange(send.reshape(members, CAP, PAIRS, LANES), ROWS).reshape(members * CAP, PAIRS, LANES)

    lists, spread = call(
        functools.partial(lists_kernel, members, groups),
        "lists",
        [vmem] * 4,
        (ints(SLOT_DEV, LANES), jax.ShapeDtypeStruct((QUARTERS * SLOT_DEV, members * CAP2 * QUARTERS), BF16)),
        [],
        0.1,
        (vmem, vmem),
    )(*entry, asked)
    work, near = call(
        functools.partial(near_kernel, per_row),
        "near",
        [smem, vmem, vmem, vmem, vmem, vmem],
        (blocks(entries + rows), blocks(SPARE, F32)),
        [
            pltpu.VMEM((3 * rows, PAIRS, LANES), BF16),
            pltpu.VMEM((2, (PAIRS + 1) * per_row, LANES), F32),
            pltpu.VMEM(((PAIRS + 1) * rows, LANES), F32),
            pltpu.VMEM((members * CAP2 + 1, PAIRS, LANES), F32),
            pltpu.SemaphoreType.DMA,
        ],
        0.1,
        (vmem, hbm),
        WIDE_LIMIT,
    )(lists, a_blocks, p_blocks, pq, low, high)
    sums = call(
        functools.partial(far_kernel, per_row),
        "far",
        [vmem, vmem, vmem, hbm],
        jax.ShapeDtypeStruct((members, CAP2 * QUARTERS, area // QUARTERS), BF16),
        [
            pltpu.VMEM((members * CAP2 + 1, PAIRS, LANES), F32),
            pltpu.SMEM((SLOT_DEV, LANES), jnp.int32),
            pltpu.SemaphoreType.DMA((2,)),
        ],
        6,
        limit=WIDE_LIMIT,
    )(lists, work, got, near)
    parts = exchange(sums, SUMS).reshape(-1, area // QUARTERS)

    return call(
        sum_kernel, "holders", [vmem, vmem], jax.ShapeDtypeStruct((SLOT_DEV, area), F32), [], 2
    )(spread, parts)


def solution(mesh):
    placed = (
        P(("grp", "row"), None, None),
        P(("grp", "row"), None),
        P(("grp", "row"), None),
        P(("grp", "row")),
        P(("grp", "row"), None),
    )
    return jax.shard_map(
        body, mesh=mesh, in_specs=placed, out_specs=P(("grp", "row"), None), check_vma=False
    )
```

```python
import functools

import jax
import jax.numpy as jnp
from jax import lax
from jax.experimental import pallas as pl
from jax.experimental.pallas import tpu as pltpu
from jax.sharding import PartitionSpec as P

BS = 64
LANES = 128
PAIRS = 32
CAP = 4
SLOT_DEV = 8
CAP2 = 4
COUNTS = 6
STEPS = (64, 32)
ASK = SUMS = tuple(reversed(range(32)))
ROWS = tuple(range(32))
PARTS = 4
QUARTERS = 4
VMEM_LIMIT = 12 * 1024 * 1024
WIDE_LIMIT = 40 * 1024 * 1024
PLAN_LIMIT = 60 * 1024 * 1024
SPARE = 1664
BF16 = jnp.bfloat16
F32 = jnp.float32


def lane_of(shape):
    return lax.broadcasted_iota(jnp.int32, shape, len(shape) - 1)


def row_of(shape):
    return lax.broadcasted_iota(jnp.int32, shape, len(shape) - 2)


def ones(mask):
    return jnp.where(mask, 1.0, 0.0).astype(BF16)


def dot(a, b, contract):
    return lax.dot_general(a, b, ((contract[:1], contract[1:]), ((), ())), preferred_element_type=F32)


def table_of(owner, local, keep, members, width):
    per_row, rows = owner.shape
    counts = jnp.zeros((members, width), F32)
    for k in range(per_row):
        of_owner = ones((row_of((members, rows)) == owner[k : k + 1]) & keep[k : k + 1])
        of_local = ones(row_of((width, rows)) == local[k : k + 1])
        counts += dot(of_owner, of_local, (1, 1))
    present = counts > 0.5
    before = ones(row_of((width, width)) < lane_of((width, width)))
    return present, dot(ones(present), before, (1, 0))


def rank_of(owner, local, rank):
    per_row, rows = owner.shape
    members, width = rank.shape
    result = jnp.zeros((per_row, rows), jnp.int32)
    for k in range(per_row):
        of_owner = ones(row_of((members, rows)) == owner[k : k + 1])
        ranks = dot(rank.astype(BF16), of_owner, (0, 0))
        mine = jnp.sum(jnp.where(row_of((width, rows)) == local[k : k + 1], ranks, 0.0), axis=0, keepdims=True)
        result = jnp.where(row_of((per_row, rows)) == k, mine.astype(jnp.int32), result)
    return result


def chosen(present, rank, cap, first, result):
    members, width = present.shape
    ids, lanes = lane_of((members, width)), lane_of((members, LANES))
    for s in range(cap):
        one = jnp.sum(jnp.where(present & (rank == float(s)), ids, 0), axis=1, keepdims=True)
        result = jnp.where(lanes == first + s, one, result)
    return result


def place_in(order, member):
    natural = tuple(range(len(order)))
    if order == natural:
        return member
    if order == natural[::-1]:
        return len(order) - 1 - member
    result = jnp.zeros_like(member)
    for at, who in enumerate(order):
        result = jnp.where(member == who, at, result)
    return result


def exchange(x, order):
    return lax.all_to_all(x, "row", 0, 0, tiled=True, axis_index_groups=[list(order)])


def split_cols(cols, rows, members):
    device_of = cols // rows
    return cols % rows, device_of // members, device_of % members


def plan_kernel(members, cols_ref, count_ref, slot_ref, want_ref):
    per_row, rows = cols_ref.shape
    local, group, member = split_cols(cols_ref[...], rows, members)
    live = row_of((per_row, rows)) < count_ref[...]
    slots = slot_ref[...]
    wanted = live & (group == lax.axis_index("grp")) & (member != lax.axis_index("row"))
    present, rank = table_of(place_in(ASK, member), local, wanted, members, rows)
    want = chosen(present, rank, CAP, 0, jnp.zeros((members, LANES), jnp.int32))
    holder = place_in(ASK, slots // SLOT_DEV % members)
    present, rank = table_of(holder, slots % SLOT_DEV, live, members, SLOT_DEV)
    want_ref[...] = chosen(present, rank, CAP2, CAP, want)


def lists_kernel(members, groups, cols_ref, count_ref, slot_ref, asked_ref, lists_ref, spread_ref):
    places = members * CAP2 * QUARTERS
    sender = lane_of((members, places)) // (CAP2 * QUARTERS)
    from_member = jnp.zeros((members, places), jnp.bool_)
    for at, who in enumerate(SUMS):
        from_member = from_member | ((sender == at) & (row_of((members, places)) == ASK.index(who)))
    from_member = ones(from_member)
    names = asked_ref[...][:, :SLOT_DEV].astype(F32).astype(BF16)
    named = dot(names, from_member, (0, 0))
    at = lane_of((SLOT_DEV, places))
    mine = row_of((SLOT_DEV, places)) == CAP + at // QUARTERS % CAP2
    slot_at = jnp.sum(jnp.where(mine, named, 0.0), axis=0, keepdims=True).astype(jnp.int32)
    at, to = lane_of((QUARTERS * SLOT_DEV, places)), row_of((QUARTERS * SLOT_DEV, places))
    spread_ref[...] = ones((to % SLOT_DEV == slot_at) & (to // SLOT_DEV == at % QUARTERS))

    per_row, rows = cols_ref.shape
    entries = per_row * rows
    at_k = row_of((per_row, rows))
    local, group, member = split_cols(cols_ref[...], rows, members)
    live = at_k < count_ref[...]
    slots = slot_ref[...]
    group_at = lax.axis_index("grp")
    in_group = group == group_at
    far = in_group & (member != lax.axis_index("row"))
    _, rank = table_of(member, local, live & far, members, rows)
    far_source = place_in(ROWS, member) * CAP + jnp.clip(rank_of(member, local, rank), 0, CAP - 1)
    low = group == lax.rem(group_at + groups - 1, groups)
    near_source = jnp.where(in_group, local, jnp.where(low, rows + local, 2 * rows + local))
    source = jnp.where(far, far_source, near_source)

    owner, slot = slots // SLOT_DEV % members, slots % SLOT_DEV
    _, rank = table_of(owner, slot, live, members, SLOT_DEV)
    target = place_in(SUMS, owner) * CAP2 + jnp.clip(rank_of(owner, slot, rank), 0, CAP2 - 1)

    entry = lane_of((per_row, rows)) * per_row + at_k
    before = ones(row_of((rows, rows)) < lane_of((rows, rows)))
    above = ones(lane_of((per_row, per_row)) < row_of((per_row, per_row)))
    halves = entries // LANES
    result = jnp.zeros((SLOT_DEV, LANES), jnp.int32)
    for which, mask in enumerate((live & ~far, live & far)):
        inside = dot(ones(mask), before, (1, 0))
        totals = jnp.sum(jnp.where(mask, 1.0, 0.0), axis=1, keepdims=True)
        earlier = dot(above, jnp.broadcast_to(totals, (per_row, LANES)).astype(BF16), (1, 0))[:, :1]
        at = jnp.where(mask, (inside + earlier).astype(jnp.int32), -1)
        count = jnp.sum(totals, axis=0, keepdims=True).astype(jnp.int32)
        placed = jnp.zeros((SLOT_DEV, entries), F32)
        for k in range(per_row):
            here = ones(row_of((entries, rows)) == at[k : k + 1])
            kind = row_of((SLOT_DEV, rows))
            value = jnp.where(kind == 0, entry[k : k + 1], jnp.where(kind == 1, source[k : k + 1], target[k : k + 1]))
            placed += dot(value.astype(F32).astype(BF16), here, (1, 1))
        placed = placed.astype(jnp.int32)
        code = placed[:1] * 65536 + placed[1:2] * 256 + placed[2:3]
        lanes = lane_of((1, entries))
        code = jnp.where(lanes < count, code, members * CAP2)
        kind = row_of((SLOT_DEV, LANES))
        for half in range(halves):
            part = code[:, half * LANES : (half + 1) * LANES]
            result = jnp.where(kind == which * halves + half, part, result)
        result = jnp.where(kind == COUNTS + which, count, result)
    lists_ref[...] = result


def prepare_kernel(p_ref, pq_ref, stage):
    rows = p_ref.shape[0]
    left = lane_of((rows, LANES)) < BS
    for h in range(PAIRS // 2):
        a = p_ref[:, h * LANES : (h + 1) * LANES].astype(F32)
        b = p_ref[:, (h + PAIRS // 2) * LANES : (h + PAIRS // 2 + 1) * LANES].astype(F32)
        stage[pl.ds(2 * h * rows, rows), :] = jnp.where(left, a, pltpu.roll(b, BS, 1))
        stage[pl.ds((2 * h + 1) * rows, rows), :] = jnp.where(left, pltpu.roll(a, BS, 1), b)
    for j in range(rows):
        pq_ref[j] = stage[pl.ds(j, PAIRS, stride=rows), :].astype(BF16)


def relay(a_ref, p_ref, pairs_ref, own_ref, stage, own_stage):
    rows, per_row, _ = a_ref.shape
    row_at, lane_at = row_of((LANES, LANES)), lane_of((LANES, LANES))
    col_at = row_at % BS
    order = (col_at % 2) * BS + (row_at // BS) * (BS // 2) + col_at // 2
    shuffle = ones(lane_at == order)
    for r in range(PAIRS):
        own_stage[pl.ds(r * rows, rows), :] = jnp.dot(
            p_ref[:, r * LANES : (r + 1) * LANES], shuffle, preferred_element_type=F32
        )
    at_once = LANES // PAIRS
    for first in range(0, rows, at_once):
        turned = jnp.concatenate(
            [own_stage[pl.ds(first + j, PAIRS, stride=rows), :] for j in range(at_once)], axis=0
        ).T
        for j in range(at_once):
            mine = turned[:, j * PAIRS : (j + 1) * PAIRS]
            own_ref[first + j] = jnp.concatenate(
                [mine[n * PAIRS : (n + 1) * PAIRS] for n in range(at_once)], axis=1
            ).astype(BF16)

    def one(i, carry):
        at = lax.rem(i, 2)
        for r in range(PAIRS):
            stage[at, pl.ds(r * per_row, per_row), :] = a_ref[i, :, r * LANES : (r + 1) * LANES].astype(F32)
        for k in range(per_row):
            pairs_ref[i * per_row + k] = stage[at, pl.ds(k, PAIRS, stride=per_row), :].astype(BF16)
        return carry

    lax.fori_loop(0, rows, one, 0, unroll=2)


def twice(block):
    left, zero = lane_of(block.shape) < BS, jnp.zeros(block.shape, block.dtype)
    swap = jnp.concatenate([block[:, BS:], block[:, :BS]], axis=1)
    parts = [
        jnp.where(left, block, zero),
        jnp.where(left, swap, zero),
        jnp.where(left, zero, swap),
        jnp.where(left, zero, block),
    ]
    return jnp.concatenate(parts, axis=0)


def two_products(lefts, rights):
    both = jnp.dot(
        jnp.concatenate(lefts, axis=0), jnp.concatenate(rights, axis=1), preferred_element_type=F32
    )
    return [both[:PAIRS, :LANES], both[PAIRS:, LANES:]]


def add_tiles(lists_ref, which, per_row, table_ref, pairs_ref, own_ref, total_ref):
    count = lists_ref[COUNTS + which, 0]
    first = which * (pairs_ref.shape[0] // LANES)

    def step(start, group):
        row, lane = first + start // LANES, lax.rem(start, LANES)
        codes = [lists_ref[row, lane + n] for n in range(group)]
        halves, tiles = [], []
        for n in range(0, group, 2):
            rights = [twice(table_ref[(code >> 8) & 255]) for code in codes[n : n + 2]]
            halves += two_products([pairs_ref[code >> 16] for code in codes[n : n + 2]], rights)
        for n in range(0, group, 2):
            rights = [twice(half.astype(BF16)) for half in halves[n : n + 2]]
            tiles += two_products([own_ref[(code >> 16) // per_row] for code in codes[n : n + 2]], rights)
        for code, tile in zip(codes, tiles):
            total_ref[code & 255] += tile

    large, small = STEPS
    whole = (count + large - 1 - small) // large
    rest = jnp.maximum(count - whole * large, 0)

    def one_large(n, carry):
        step(n * large, large)
        return carry

    def one_small(n, carry):
        step(whole * large + n * small, small)
        return carry

    lax.fori_loop(0, whole, one_large, 0)
    lax.fori_loop(0, (rest + small - 1) // small, one_small, 0)


def views(work_ref, per_row):
    entries = work_ref.shape[0] // (per_row + 1) * per_row
    return work_ref.at[pl.ds(0, entries)], work_ref.at[pl.ds(entries, entries // per_row)]


def clear(total_ref):
    def one(at, carry):
        total_ref[at] = jnp.zeros((PAIRS, LANES), F32)
        return carry

    lax.fori_loop(0, total_ref.shape[0], one, 0, unroll=8)


def near_kernel(per_row, lists_ref, a_ref, p_ref, pq_ref, low_ref, high_ref, work_ref, near_ref,
                table, stage, own_stage, total_ref, sem):
    pairs_ref, own_ref = views(work_ref, per_row)
    relay(a_ref, p_ref, pairs_ref, own_ref, stage, own_stage)
    rows = pq_ref.shape[0]
    for at, ref in enumerate((pq_ref, low_ref, high_ref)):
        table[pl.ds(at * rows, rows)] = ref[...]
    clear(total_ref)
    add_tiles(lists_ref, 0, per_row, table, pairs_ref, own_ref, total_ref)
    sums = total_ref.shape[0] - 1
    copy = pltpu.make_async_copy(total_ref.at[pl.ds(0, sums)], near_ref.at[pl.ds(0, sums)], sem)
    copy.start()
    copy.wait()


def far_kernel(per_row, lists_from, work_ref, got_ref, near_ref, out_ref, total, lists_ref, sem):
    blocks = total.shape[0] - 1
    copies = [
        pltpu.make_async_copy(near_ref.at[pl.ds(0, blocks)], total.at[pl.ds(0, blocks)], sem.at[0]),
        pltpu.make_async_copy(lists_from, lists_ref, sem.at[1]),
    ]
    for copy in copies:
        copy.start()
    total[blocks] = jnp.zeros((PAIRS, LANES), F32)
    pairs_ref, own_ref = views(work_ref, per_row)
    for copy in copies:
        copy.wait()
    add_tiles(lists_ref, 1, per_row, got_ref, pairs_ref, own_ref, total)
    for member in range(out_ref.shape[0]):
        for at in range(PAIRS // QUARTERS):
            rows = total.at[pl.ds(member * CAP2, CAP2)].reshape(CAP2 * PAIRS, LANES)[
                pl.ds(at, CAP2 * QUARTERS, stride=PAIRS // QUARTERS), :
            ]
            out_ref[member, :, at * LANES : (at + 1) * LANES] = rows.astype(BF16)


def pack_kernel(members, asked_from, pq_ref, out_ref, asked_ref, sem):
    share = members // PARTS
    copies = [
        pltpu.make_async_copy(
            asked_from.at[pl.ds(n * share, share)], asked_ref.at[pl.ds(n * share, share)], sem.at[n]
        )
        for n in range(PARTS)
    ]
    for copy in copies:
        copy.start()
    for n, copy in enumerate(copies):
        copy.wait()
        for row in range(n * share, (n + 1) * share):
            at = ROWS.index(ASK[row])
            for s in range(CAP):
                out_ref[at * CAP + s] = pq_ref[asked_ref[row, s]]


def sum_kernel(spread_ref, got_ref, out_ref):
    result = jnp.dot(spread_ref[...], got_ref[...], preferred_element_type=F32)
    width = got_ref.shape[1]
    for n in range(QUARTERS):
        out_ref[:, n * width : (n + 1) * width] = result[n * SLOT_DEV : (n + 1) * SLOT_DEV]


def body(a_blocks, p_blocks, a_cols, a_count, tile_slot):
    rows, per_row, area = a_blocks.shape
    members = lax.axis_size("row")
    groups = lax.axis_size("grp")
    entries = rows * per_row
    smem = pl.BlockSpec(memory_space=pltpu.SMEM)
    vmem = pl.BlockSpec(memory_space=pltpu.VMEM)
    hbm = pl.BlockSpec(memory_space=pltpu.HBM)
    blocks = lambda n, dtype=BF16: jax.ShapeDtypeStruct((n, PAIRS, LANES), dtype)
    ints = lambda *shape: jax.ShapeDtypeStruct(shape, jnp.int32)

    def call(kernel, name, ins, outs, scratch, us, out_specs=vmem, limit=VMEM_LIMIT):
        return pl.pallas_call(
            kernel,
            out_shape=outs,
            in_specs=ins,
            out_specs=out_specs,
            scratch_shapes=scratch,
            compiler_params=pltpu.CompilerParams(vmem_limit_bytes=limit),
            cost_estimate=pl.CostEstimate(flops=0, bytes_accessed=int(us * 3e6), transcendentals=0),
            name=name,
        )

    entry = (a_cols.T, a_count.reshape(1, rows), tile_slot.T)
    want = call(
        functools.partial(plan_kernel, members), "plan", [vmem] * 3, ints(members, LANES), [], 2, limit=PLAN_LIMIT
    )(*entry)
    asked = exchange(want.reshape(members, 1, LANES), ASK).reshape(members, LANES)

    pq = call(
        prepare_kernel, "prepare", [vmem], blocks(rows), [pltpu.VMEM(((PAIRS + 1) * rows, LANES), F32)], 0.1
    )(p_blocks)
    forward = [(i, (i + 1) % groups) for i in range(groups)]
    low = lax.ppermute(pq, "grp", forward)
    high = lax.ppermute(pq, "grp", [(target, source) for source, target in forward])

    send = call(
        functools.partial(pack_kernel, members), "pack", [vmem, vmem], blocks(members * CAP),
        [pltpu.SMEM((members, LANES), jnp.int32), pltpu.SemaphoreType.DMA((PARTS,))], 2
    )(asked, pq)
    got = exchange(send.reshape(members, CAP, PAIRS, LANES), ROWS).reshape(members * CAP, PAIRS, LANES)

    lists, spread = call(
        functools.partial(lists_kernel, members, groups),
        "lists",
        [vmem] * 4,
        (ints(SLOT_DEV, LANES), jax.ShapeDtypeStruct((QUARTERS * SLOT_DEV, members * CAP2 * QUARTERS), BF16)),
        [],
        0.1,
        (vmem, vmem),
    )(*entry, asked)
    work, near = call(
        functools.partial(near_kernel, per_row),
        "near",
        [smem, vmem, vmem, vmem, vmem, vmem],
        (blocks(entries + rows), blocks(SPARE, F32)),
        [
            pltpu.VMEM((3 * rows, PAIRS, LANES), BF16),
            pltpu.VMEM((2, (PAIRS + 1) * per_row, LANES), F32),
            pltpu.VMEM(((PAIRS + 1) * rows, LANES), F32),
            pltpu.VMEM((members * CAP2 + 1, PAIRS, LANES), F32),
            pltpu.SemaphoreType.DMA,
        ],
        0.1,
        (vmem, hbm),
        WIDE_LIMIT,
    )(lists, a_blocks, p_blocks, pq, low, high)
    sums = call(
        functools.partial(far_kernel, per_row),
        "far",
        [vmem, vmem, vmem, hbm],
        jax.ShapeDtypeStruct((members, CAP2 * QUARTERS, area // QUARTERS), BF16),
        [
            pltpu.VMEM((members * CAP2 + 1, PAIRS, LANES), F32),
            pltpu.SMEM((SLOT_DEV, LANES), jnp.int32),
            pltpu.SemaphoreType.DMA((2,)),
        ],
        6,
        limit=WIDE_LIMIT,
    )(lists, work, got, near)
    parts = exchange(sums, SUMS).reshape(-1, area // QUARTERS)

    return call(
        sum_kernel, "holders", [vmem, vmem], jax.ShapeDtypeStruct((SLOT_DEV, area), F32), [], 2
    )(spread, parts)


def solution(mesh):
    placed = (
        P(("grp", "row"), None, None),
        P(("grp", "row"), None),
        P(("grp", "row"), None),
        P(("grp", "row")),
        P(("grp", "row"), None),
    )
    return jax.shard_map(
        body, mesh=mesh, in_specs=placed, out_specs=P(("grp", "row"), None), check_vma=False
    )
```

```python
import functools

import jax
import jax.numpy as jnp
from jax import lax
from jax.experimental import pallas as pl
from jax.experimental.pallas import tpu as pltpu
from jax.sharding import PartitionSpec as P

BS = 64
LANES = 128
PAIRS = 32
CAP = 4
SLOT_DEV = 8
CAP2 = 4
COUNTS = 6
STEPS = (128, 64)
ASK = SUMS = tuple(reversed(range(32)))
ROWS = tuple(range(32))
PARTS = 4
QUARTERS = 4
VMEM_LIMIT = 12 * 1024 * 1024
WIDE_LIMIT = 40 * 1024 * 1024
PLAN_LIMIT = 60 * 1024 * 1024
SPARE = 1664
BF16 = jnp.bfloat16
F32 = jnp.float32


def lane_of(shape):
    return lax.broadcasted_iota(jnp.int32, shape, len(shape) - 1)


def row_of(shape):
    return lax.broadcasted_iota(jnp.int32, shape, len(shape) - 2)


def ones(mask):
    return jnp.where(mask, 1.0, 0.0).astype(BF16)


def dot(a, b, contract):
    return lax.dot_general(a, b, ((contract[:1], contract[1:]), ((), ())), preferred_element_type=F32)


def table_of(owner, local, keep, members, width):
    per_row, rows = owner.shape
    counts = jnp.zeros((members, width), F32)
    for k in range(per_row):
        of_owner = ones((row_of((members, rows)) == owner[k : k + 1]) & keep[k : k + 1])
        of_local = ones(row_of((width, rows)) == local[k : k + 1])
        counts += dot(of_owner, of_local, (1, 1))
    present = counts > 0.5
    before = ones(row_of((width, width)) < lane_of((width, width)))
    return present, dot(ones(present), before, (1, 0))


def rank_of(owner, local, rank):
    per_row, rows = owner.shape
    members, width = rank.shape
    result = jnp.zeros((per_row, rows), jnp.int32)
    for k in range(per_row):
        of_owner = ones(row_of((members, rows)) == owner[k : k + 1])
        ranks = dot(rank.astype(BF16), of_owner, (0, 0))
        mine = jnp.sum(jnp.where(row_of((width, rows)) == local[k : k + 1], ranks, 0.0), axis=0, keepdims=True)
        result = jnp.where(row_of((per_row, rows)) == k, mine.astype(jnp.int32), result)
    return result


def chosen(present, rank, cap, first, result):
    members, width = present.shape
    ids, lanes = lane_of((members, width)), lane_of((members, LANES))
    for s in range(cap):
        one = jnp.sum(jnp.where(present & (rank == float(s)), ids, 0), axis=1, keepdims=True)
        result = jnp.where(lanes == first + s, one, result)
    return result


def place_in(order, member):
    result = jnp.zeros_like(member)
    for at, who in enumerate(order):
        result = jnp.where(member == who, at, result)
    return result


def exchange(x, order):
    return lax.all_to_all(x, "row", 0, 0, tiled=True, axis_index_groups=[list(order)])


def split_cols(cols, rows, members):
    device_of = cols // rows
    return cols % rows, device_of // members, device_of % members


def plan_kernel(members, cols_ref, count_ref, slot_ref, want_ref):
    per_row, rows = cols_ref.shape
    local, group, member = split_cols(cols_ref[...], rows, members)
    live = row_of((per_row, rows)) < count_ref[...]
    slots = slot_ref[...]
    wanted = live & (group == lax.axis_index("grp")) & (member != lax.axis_index("row"))
    present, rank = table_of(place_in(ASK, member), local, wanted, members, rows)
    want = chosen(present, rank, CAP, 0, jnp.zeros((members, LANES), jnp.int32))
    holder = place_in(ASK, slots // SLOT_DEV % members)
    present, rank = table_of(holder, slots % SLOT_DEV, live, members, SLOT_DEV)
    want_ref[...] = chosen(present, rank, CAP2, CAP, want)


def lists_kernel(members, groups, cols_ref, count_ref, slot_ref, asked_ref, lists_ref, spread_ref):
    places = members * CAP2 * QUARTERS
    sender = lane_of((members, places)) // (CAP2 * QUARTERS)
    from_member = jnp.zeros((members, places), jnp.bool_)
    for at, who in enumerate(SUMS):
        from_member = from_member | ((sender == at) & (row_of((members, places)) == ASK.index(who)))
    from_member = ones(from_member)
    names = asked_ref[...][:, :SLOT_DEV].astype(F32).astype(BF16)
    named = dot(names, from_member, (0, 0))
    at = lane_of((SLOT_DEV, places))
    mine = row_of((SLOT_DEV, places)) == CAP + at // QUARTERS % CAP2
    slot_at = jnp.sum(jnp.where(mine, named, 0.0), axis=0, keepdims=True).astype(jnp.int32)
    at, to = lane_of((QUARTERS * SLOT_DEV, places)), row_of((QUARTERS * SLOT_DEV, places))
    spread_ref[...] = ones((to % SLOT_DEV == slot_at) & (to // SLOT_DEV == at % QUARTERS))

    per_row, rows = cols_ref.shape
    entries = per_row * rows
    at_k = row_of((per_row, rows))
    local, group, member = split_cols(cols_ref[...], rows, members)
    live = at_k < count_ref[...]
    slots = slot_ref[...]
    group_at = lax.axis_index("grp")
    in_group = group == group_at
    far = in_group & (member != lax.axis_index("row"))
    _, rank = table_of(member, local, live & far, members, rows)
    far_source = place_in(ROWS, member) * CAP + jnp.clip(rank_of(member, local, rank), 0, CAP - 1)
    low = group == lax.rem(group_at + groups - 1, groups)
    near_source = jnp.where(in_group, local, jnp.where(low, rows + local, 2 * rows + local))
    source = jnp.where(far, far_source, near_source)

    owner, slot = slots // SLOT_DEV % members, slots % SLOT_DEV
    _, rank = table_of(owner, slot, live, members, SLOT_DEV)
    target = place_in(SUMS, owner) * CAP2 + jnp.clip(rank_of(owner, slot, rank), 0, CAP2 - 1)

    entry = lane_of((per_row, rows)) * per_row + at_k
    before = ones(row_of((rows, rows)) < lane_of((rows, rows)))
    above = ones(lane_of((per_row, per_row)) < row_of((per_row, per_row)))
    halves = entries // LANES
    result = jnp.zeros((SLOT_DEV, LANES), jnp.int32)
    for which, mask in enumerate((live & ~far, live & far)):
        inside = dot(ones(mask), before, (1, 0))
        totals = jnp.sum(jnp.where(mask, 1.0, 0.0), axis=1, keepdims=True)
        earlier = dot(above, jnp.broadcast_to(totals, (per_row, LANES)).astype(BF16), (1, 0))[:, :1]
        at = jnp.where(mask, (inside + earlier).astype(jnp.int32), -1)
        count = jnp.sum(totals, axis=0, keepdims=True).astype(jnp.int32)
        placed = jnp.zeros((SLOT_DEV, entries), F32)
        for k in range(per_row):
            here = ones(row_of((entries, rows)) == at[k : k + 1])
            kind = row_of((SLOT_DEV, rows))
            value = jnp.where(kind == 0, entry[k : k + 1], jnp.where(kind == 1, source[k : k + 1], target[k : k + 1]))
            placed += dot(value.astype(F32).astype(BF16), here, (1, 1))
        placed = placed.astype(jnp.int32)
        code = placed[:1] * 65536 + placed[1:2] * 256 + placed[2:3]
        lanes = lane_of((1, entries))
        code = jnp.where(lanes < count, code, members * CAP2)
        kind = row_of((SLOT_DEV, LANES))
        for half in range(halves):
            part = code[:, half * LANES : (half + 1) * LANES]
            result = jnp.where(kind == which * halves + half, part, result)
        result = jnp.where(kind == COUNTS + which, count, result)
    lists_ref[...] = result


def prepare_kernel(p_ref, pq_ref, stage):
    rows = p_ref.shape[0]
    left = lane_of((rows, LANES)) < BS
    for h in range(PAIRS // 2):
        a = p_ref[:, h * LANES : (h + 1) * LANES].astype(F32)
        b = p_ref[:, (h + PAIRS // 2) * LANES : (h + PAIRS // 2 + 1) * LANES].astype(F32)
        stage[pl.ds(2 * h * rows, rows), :] = jnp.where(left, a, pltpu.roll(b, BS, 1))
        stage[pl.ds((2 * h + 1) * rows, rows), :] = jnp.where(left, pltpu.roll(a, BS, 1), b)
    for j in range(rows):
        pq_ref[j] = stage[pl.ds(j, PAIRS, stride=rows), :].astype(BF16)


def relay(a_ref, p_ref, pairs_ref, own_ref, stage, own_stage):
    rows, per_row, _ = a_ref.shape
    row_at, lane_at = row_of((LANES, LANES)), lane_of((LANES, LANES))
    col_at = row_at % BS
    order = (col_at % 2) * BS + (row_at // BS) * (BS // 2) + col_at // 2
    shuffle = ones(lane_at == order)
    for r in range(PAIRS):
        own_stage[pl.ds(r * rows, rows), :] = jnp.dot(
            p_ref[:, r * LANES : (r + 1) * LANES], shuffle, preferred_element_type=F32
        )
    at_once = LANES // PAIRS
    for first in range(0, rows, at_once):
        turned = jnp.concatenate(
            [own_stage[pl.ds(first + j, PAIRS, stride=rows), :] for j in range(at_once)], axis=0
        ).T
        for j in range(at_once):
            mine = turned[:, j * PAIRS : (j + 1) * PAIRS]
            own_ref[first + j] = jnp.concatenate(
                [mine[n * PAIRS : (n + 1) * PAIRS] for n in range(at_once)], axis=1
            ).astype(BF16)

    def one(i, carry):
        at = lax.rem(i, 2)
        for r in range(PAIRS):
            stage[at, pl.ds(r * per_row, per_row), :] = a_ref[i, :, r * LANES : (r + 1) * LANES].astype(F32)
        for k in range(per_row):
            pairs_ref[i * per_row + k] = stage[at, pl.ds(k, PAIRS, stride=per_row), :].astype(BF16)
        return carry

    lax.fori_loop(0, rows, one, 0, unroll=2)


def twice(block):
    left, zero = lane_of(block.shape) < BS, jnp.zeros(block.shape, block.dtype)
    swap = jnp.concatenate([block[:, BS:], block[:, :BS]], axis=1)
    parts = [
        jnp.where(left, block, zero),
        jnp.where(left, swap, zero),
        jnp.where(left, zero, swap),
        jnp.where(left, zero, block),
    ]
    return jnp.concatenate(parts, axis=0)


def two_products(lefts, rights):
    both = jnp.dot(
        jnp.concatenate(lefts, axis=0), jnp.concatenate(rights, axis=1), preferred_element_type=F32
    )
    return [both[:PAIRS, :LANES], both[PAIRS:, LANES:]]


def add_tiles(lists_ref, which, per_row, table_ref, pairs_ref, own_ref, total_ref):
    count = lists_ref[COUNTS + which, 0]
    first = which * (pairs_ref.shape[0] // LANES)

    def step(start, group):
        row, lane = first + start // LANES, lax.rem(start, LANES)
        codes = [lists_ref[row, lane + n] for n in range(group)]
        halves, tiles = [], []
        for n in range(0, group, 2):
            rights = [twice(table_ref[(code >> 8) & 255]) for code in codes[n : n + 2]]
            halves += two_products([pairs_ref[code >> 16] for code in codes[n : n + 2]], rights)
        for n in range(0, group, 2):
            rights = [twice(half.astype(BF16)) for half in halves[n : n + 2]]
            tiles += two_products([own_ref[(code >> 16) // per_row] for code in codes[n : n + 2]], rights)
        for code, tile in zip(codes, tiles):
            total_ref[code & 255] += tile

    large, small = STEPS
    whole = (count + large - 1 - small) // large
    rest = jnp.maximum(count - whole * large, 0)

    def one_large(n, carry):
        step(n * large, large)
        return carry

    def one_small(n, carry):
        step(whole * large + n * small, small)
        return carry

    lax.fori_loop(0, whole, one_large, 0)
    lax.fori_loop(0, (rest + small - 1) // small, one_small, 0)


def views(work_ref, per_row):
    entries = work_ref.shape[0] // (per_row + 1) * per_row
    return work_ref.at[pl.ds(0, entries)], work_ref.at[pl.ds(entries, entries // per_row)]


def clear(total_ref):
    def one(at, carry):
        total_ref[at] = jnp.zeros((PAIRS, LANES), F32)
        return carry

    lax.fori_loop(0, total_ref.shape[0], one, 0, unroll=8)


def near_kernel(per_row, lists_ref, a_ref, p_ref, pq_ref, low_ref, high_ref, work_ref, near_ref,
                table, stage, own_stage, total_ref, sem):
    pairs_ref, own_ref = views(work_ref, per_row)
    relay(a_ref, p_ref, pairs_ref, own_ref, stage, own_stage)
    rows = pq_ref.shape[0]
    for at, ref in enumerate((pq_ref, low_ref, high_ref)):
        table[pl.ds(at * rows, rows)] = ref[...]
    clear(total_ref)
    add_tiles(lists_ref, 0, per_row, table, pairs_ref, own_ref, total_ref)
    sums = total_ref.shape[0] - 1
    copy = pltpu.make_async_copy(total_ref.at[pl.ds(0, sums)], near_ref.at[pl.ds(0, sums)], sem)
    copy.start()
    copy.wait()


def far_kernel(per_row, lists_from, work_ref, got_ref, near_ref, out_ref, total, lists_ref, sem):
    blocks = total.shape[0] - 1
    copies = [
        pltpu.make_async_copy(near_ref.at[pl.ds(0, blocks)], total.at[pl.ds(0, blocks)], sem.at[0]),
        pltpu.make_async_copy(lists_from, lists_ref, sem.at[1]),
    ]
    for copy in copies:
        copy.start()
    total[blocks] = jnp.zeros((PAIRS, LANES), F32)
    pairs_ref, own_ref = views(work_ref, per_row)
    for copy in copies:
        copy.wait()
    add_tiles(lists_ref, 1, per_row, got_ref, pairs_ref, own_ref, total)
    for member in range(out_ref.shape[0]):
        for at in range(PAIRS // QUARTERS):
            rows = total.at[pl.ds(member * CAP2, CAP2)].reshape(CAP2 * PAIRS, LANES)[
                pl.ds(at, CAP2 * QUARTERS, stride=PAIRS // QUARTERS), :
            ]
            out_ref[member, :, at * LANES : (at + 1) * LANES] = rows.astype(BF16)


def pack_kernel(members, asked_from, pq_ref, out_ref, asked_ref, sem):
    share = members // PARTS
    copies = [
        pltpu.make_async_copy(
            asked_from.at[pl.ds(n * share, share)], asked_ref.at[pl.ds(n * share, share)], sem.at[n]
        )
        for n in range(PARTS)
    ]
    for copy in copies:
        copy.start()
    for n, copy in enumerate(copies):
        copy.wait()
        for row in range(n * share, (n + 1) * share):
            at = ROWS.index(ASK[row])
            for s in range(CAP):
                out_ref[at * CAP + s] = pq_ref[asked_ref[row, s]]


def sum_kernel(spread_ref, got_ref, out_ref):
    result = jnp.dot(spread_ref[...], got_ref[...], preferred_element_type=F32)
    width = got_ref.shape[1]
    for n in range(QUARTERS):
        out_ref[:, n * width : (n + 1) * width] = result[n * SLOT_DEV : (n + 1) * SLOT_DEV]


def body(a_blocks, p_blocks, a_cols, a_count, tile_slot):
    rows, per_row, area = a_blocks.shape
    members = lax.axis_size("row")
    groups = lax.axis_size("grp")
    entries = rows * per_row
    smem = pl.BlockSpec(memory_space=pltpu.SMEM)
    vmem = pl.BlockSpec(memory_space=pltpu.VMEM)
    hbm = pl.BlockSpec(memory_space=pltpu.HBM)
    blocks = lambda n, dtype=BF16: jax.ShapeDtypeStruct((n, PAIRS, LANES), dtype)
    ints = lambda *shape: jax.ShapeDtypeStruct(shape, jnp.int32)

    def call(kernel, name, ins, outs, scratch, us, out_specs=vmem, limit=VMEM_LIMIT):
        return pl.pallas_call(
            kernel,
            out_shape=outs,
            in_specs=ins,
            out_specs=out_specs,
            scratch_shapes=scratch,
            compiler_params=pltpu.CompilerParams(vmem_limit_bytes=limit),
            cost_estimate=pl.CostEstimate(flops=0, bytes_accessed=int(us * 3e6), transcendentals=0),
            name=name,
        )

    entry = (a_cols.T, a_count.reshape(1, rows), tile_slot.T)
    want = call(
        functools.partial(plan_kernel, members), "plan", [vmem] * 3, ints(members, LANES), [], 2, limit=PLAN_LIMIT
    )(*entry)
    asked = exchange(want.reshape(members, 1, LANES), ASK).reshape(members, LANES)

    pq = call(
        prepare_kernel, "prepare", [vmem], blocks(rows), [pltpu.VMEM(((PAIRS + 1) * rows, LANES), F32)], 0.1
    )(p_blocks)
    forward = [(i, (i + 1) % groups) for i in range(groups)]
    low = lax.ppermute(pq, "grp", forward)
    high = lax.ppermute(pq, "grp", [(target, source) for source, target in forward])

    send = call(
        functools.partial(pack_kernel, members), "pack", [vmem, vmem], blocks(members * CAP),
        [pltpu.SMEM((members, LANES), jnp.int32), pltpu.SemaphoreType.DMA((PARTS,))], 2
    )(asked, pq)
    got = exchange(send.reshape(members, CAP, PAIRS, LANES), ROWS).reshape(members * CAP, PAIRS, LANES)

    lists, spread = call(
        functools.partial(lists_kernel, members, groups),
        "lists",
        [vmem] * 4,
        (ints(SLOT_DEV, LANES), jax.ShapeDtypeStruct((QUARTERS * SLOT_DEV, members * CAP2 * QUARTERS), BF16)),
        [],
        0.1,
        (vmem, vmem),
    )(*entry, asked)
    work, near = call(
        functools.partial(near_kernel, per_row),
        "near",
        [smem, vmem, vmem, vmem, vmem, vmem],
        (blocks(entries + rows), blocks(SPARE, F32)),
        [
            pltpu.VMEM((3 * rows, PAIRS, LANES), BF16),
            pltpu.VMEM((2, (PAIRS + 1) * per_row, LANES), F32),
            pltpu.VMEM(((PAIRS + 1) * rows, LANES), F32),
            pltpu.VMEM((members * CAP2 + 1, PAIRS, LANES), F32),
            pltpu.SemaphoreType.DMA,
        ],
        0.1,
        (vmem, hbm),
        WIDE_LIMIT,
    )(lists, a_blocks, p_blocks, pq, low, high)
    sums = call(
        functools.partial(far_kernel, per_row),
        "far",
        [vmem, vmem, vmem, hbm],
        jax.ShapeDtypeStruct((members, CAP2 * QUARTERS, area // QUARTERS), BF16),
        [
            pltpu.VMEM((members * CAP2 + 1, PAIRS, LANES), F32),
            pltpu.SMEM((SLOT_DEV, LANES), jnp.int32),
            pltpu.SemaphoreType.DMA((2,)),
        ],
        6,
        limit=WIDE_LIMIT,
    )(lists, work, got, near)
    parts = exchange(sums, SUMS).reshape(-1, area // QUARTERS)

    return call(
        sum_kernel, "holders", [vmem, vmem], jax.ShapeDtypeStruct((SLOT_DEV, area), F32), [], 2
    )(spread, parts)


def solution(mesh):
    placed = (
        P(("grp", "row"), None, None),
        P(("grp", "row"), None),
        P(("grp", "row"), None),
        P(("grp", "row")),
        P(("grp", "row"), None),
    )
    return jax.shard_map(
        body, mesh=mesh, in_specs=placed, out_specs=P(("grp", "row"), None), check_vma=False
    )
```
